32 devices in a mesh: row: 4 (over y, x), col: 8 (over z, core).
Axes of the slice: x: 2, y: 2, z: 4, core: 2. Of those that a mesh axis runs over, the one named last changes fastest.
Arguments:
- latent: bfloat16 [64, 64, 256], P('row', 'col'), may hold values from -6 to 6
- well_logs: bfloat16 [32, 256], P(('row', 'col')), may hold values from -6 to 6
- cond_weight: bfloat16 [256, 256], replicated, may hold values from -0.375 to 0.375
- trace_rows: int32 [64], P('col'), may hold values from 0 to 31, as said below
- norm_gain: float32 [256], replicated, may hold values from 0.5 to 1.5
- in_weight: bfloat16 [256, 512], replicated, may hold values from -0.375 to 0.375
- conv_weight: float32 [9, 256], replicated, may hold values from -2 to 2
- bc_weight: bfloat16 [256, 1024], replicated, may hold values from -0.375 to 0.375
- dt_weight: bfloat16 [256, 64], replicated, may hold values from -0.375 to 0.375
- dt_bias: float32 [4, 16], replicated, may hold values from -0.5 to 0.5
- row_rate: float32 [2, 16], replicated, may hold values from 1 to 512
- col_rate: float32 [2, 16], replicated, may hold values from 1 to 512
- horizon: float32 [64, 64], P('row', 'col'), may hold values from 0 to 1
- out_gain: float32 [256], replicated, may hold values from 0.5 to 1.5
- out_weight: bfloat16 [256, 256], replicated, may hold values from -0.375 to 0.375
Outputs:
- block_out: bfloat16 [64, 64, 256], P('row', 'col')
The draws below stay inside these ranges and needn't reach their ends.
Inputs may be any that keep to these rules, and one draw needn't show every extreme that they name: `trace_rows`: every conditioning token row is named by some plane column.
All inputs are finite; a program needn't handle non-finite values.
Results may differ from the reference program's by a relative error of at most 0.009.
Values may be sent and summed in bfloat16 or wider, within the bound.
A program may use at most 192 MiB of HBM per device.

```python
import math
import jax
import jax.numpy as jnp
from jax import lax

D = 256
E = 256
HEADS = 16
STATE = 128
HEAD_DIM = 16
GRID_ROW_COUNT = 64
GRID_COLUMN_COUNT = 64
NCOND = 32


def draw_trace_rows(key, part):
    order = jax.random.permutation(key, GRID_COLUMN_COUNT)
    return (order * NCOND // GRID_COLUMN_COUNT).astype(jnp.int32)


def rate_table(key):
    key_slow = jax.random.fold_in(key, 0)
    values = jnp.exp(jax.random.uniform(key_slow, (2 * HEADS,), jnp.float32, math.log(1.0), math.log(512.0)))
    return values.reshape(2, HEADS).astype(jnp.float32)


def draw_row_rate(key, part):
    return rate_table(jax.random.fold_in(key, 11))


def draw_col_rate(key, part):
    return rate_table(jax.random.fold_in(key, 23))


def draw_horizon(key, part):
    random_seed_offset, key_spike, key_root = jax.random.split(key, 3)
    sudden_jumps = jax.random.uniform(random_seed_offset, (GRID_ROW_COUNT, GRID_COLUMN_COUNT), jnp.float32) < 1.0 / 512.0
    large_amplitude_trace = jax.random.uniform(key_spike, (GRID_ROW_COUNT, GRID_COLUMN_COUNT), jnp.float32, 0.22, 0.7)
    faint_amplitude_trace = jax.random.uniform(key_root, (GRID_ROW_COUNT, GRID_COLUMN_COUNT), jnp.float32, 0.0, 0.002)
    return jnp.where(sudden_jumps, large_amplitude_trace, faint_amplitude_trace).astype(jnp.float32)


def shard_levels(stream_key, shape, shards, low, top_value):
    factor_of = 1.0
    for dim, blocks in shards:
        steps = jax.random.uniform(jax.random.fold_in(jax.random.fold_in(stream_key, 6), dim), (blocks,), jnp.float32, low / len(shards), top_value / len(shards))
        factor_of = factor_of * jnp.repeat(jnp.exp(steps), shape[dim] // blocks).reshape((-1,) + (1,) * (len(shape) - 1 - dim))
    return factor_of


def noise(own_key, dims, width, bound, cuts=(), kind=jnp.bfloat16):
    values = jax.random.normal(own_key, dims, jnp.float32) * width
    if len(cuts) > 0:
        values = shard_levels(own_key, dims, cuts, -0.22, 0.18) * values
    return jnp.clip(values, min=-bound, max=bound).astype(kind)


def setup_inputs(seed: int = 0) -> dict:
    keys = jax.random.split(jax.random.key(seed), 16)
    latent = noise(keys[0], (GRID_ROW_COUNT, GRID_COLUMN_COUNT, D), 1.0, 6.0, ((0, 4), (1, 8)))
    well_logs = noise(keys[1], (NCOND, D), 1.0, 6.0, ((0, 32),))
    cond_weight = noise(keys[2], (D, D), D ** -0.5, 0.375)
    trace_rows = draw_trace_rows(jax.random.fold_in(keys[15], 71), 0)
    norm_gain = jnp.clip(1.0 + 0.1 * jax.random.normal(keys[4], (D,), jnp.float32), 0.5, 1.5)
    in_weight = noise(keys[5], (D, 2 * E), D ** -0.5, 0.375)
    conv_weight = noise(keys[6], (9, E), 9 ** -0.5, 2.0, (), jnp.float32)
    bc_weight = noise(keys[7], (E, 8 * STATE), E ** -0.5, 0.375)
    dt_weight = noise(keys[8], (E, 4 * HEADS), E ** -0.5, 0.375)
    dt_bias = jnp.clip(jax.random.uniform(keys[9], (4, HEADS), jnp.float32, -0.5, 0.5), -0.5, 0.5)
    row_rate = draw_row_rate(jax.random.fold_in(keys[15], 71), 0)
    col_rate = draw_col_rate(jax.random.fold_in(keys[15], 71), 0)
    horizon = draw_horizon(jax.random.fold_in(keys[15], 71), 0)
    out_gain = jnp.clip(1.0 + 0.1 * jax.random.normal(keys[13], (E,), jnp.float32), 0.5, 1.5)
    out_weight = noise(keys[14], (E, D), E ** -0.5, 0.375)
    return dict(latent=latent, well_logs=well_logs, cond_weight=cond_weight, trace_rows=trace_rows, norm_gain=norm_gain, in_weight=in_weight, conv_weight=conv_weight, bc_weight=bc_weight, dt_weight=dt_weight, dt_bias=dt_bias, row_rate=row_rate, col_rate=col_rate, horizon=horizon, out_gain=out_gain, out_weight=out_weight)


precise = lax.Precision.HIGHEST

def segment_recurrence(states, pieces):
    signal, in_coef, out_coef, step_size, log_decay = pieces
    block_len = signal.shape[1]
    cumulative = jnp.cumsum(log_decay, axis=1)
    scores = jnp.einsum('lks,ljs->lkj', out_coef, in_coef, preferred_element_type=jnp.float32)
    driven = signal.astype(jnp.float32) * step_size[..., None]
    causal = jnp.arange(block_len)[:, None] >= jnp.arange(block_len)[None, :]

    def head_term(head_args):
        head_cum, head_drive = head_args
        spread = jnp.where(causal, head_cum[:, :, None] - head_cum[:, None, :], -jnp.inf)
        return jnp.einsum('lkj,ljp->lkp', scores * jnp.exp(spread), head_drive, precision=precise)
    inner = lax.map(head_term, (jnp.moveaxis(cumulative, 2, 0), jnp.moveaxis(driven, 2, 0)))
    inner = jnp.moveaxis(inner, 0, 2)
    carried_in = jnp.exp(cumulative)[..., None] * jnp.einsum('lks,lhps->lkhp', out_coef.astype(jnp.float32), states, precision=precise)
    tail_decay = jnp.exp(cumulative[:, -1:, :] - cumulative)
    states = jnp.exp(cumulative[:, -1, :])[:, :, None, None] * states + jnp.einsum('lkhp,lks->lhps', driven * tail_decay[..., None], in_coef.astype(jnp.float32), precision=precise)
    output = inner + carried_in
    return (states, output.reshape(output.shape[0], block_len, -1))

def line_scan(signal, in_coef, out_coef, step_size, log_decay, states):
    line_count = signal.shape[0]
    length = signal.shape[1]
    block_len = min(64, length)
    blocks = length // block_len

    def split_blocks(array):
        shaped = array.reshape((line_count, blocks, block_len) + array.shape[2:])
        return jnp.moveaxis(shaped, 1, 0)
    pieces = (split_blocks(signal), split_blocks(in_coef), split_blocks(out_coef), split_blocks(step_size), split_blocks(log_decay))
    states, outputs = lax.scan(segment_recurrence, states, pieces)
    outputs = jnp.moveaxis(outputs, 0, 1).reshape(line_count, length, -1)
    return (outputs, states)

def orient(array, along_columns, backward):
    if along_columns:
        array = jnp.swapaxes(array, 0, 1)
    if backward:
        array = jnp.flip(array, 1)
    return array

def restore(array, along_columns, backward):
    if backward:
        array = jnp.flip(array, 1)
    if along_columns:
        array = jnp.swapaxes(array, 0, 1)
    return array

def reference(latent, well_logs, cond_weight, trace_rows, norm_gain, in_weight, conv_weight, bc_weight, dt_weight, dt_bias, row_rate, col_rate, horizon, out_gain, out_weight):
    tokens = jax.nn.silu(jnp.dot(well_logs, cond_weight, preferred_element_type=jnp.float32)).astype(jnp.bfloat16)
    column_tokens = jnp.take(tokens, trace_rows, axis=0).astype(jnp.float32)
    hidden = latent.astype(jnp.float32) + column_tokens[None, :, :]
    normed = (hidden * lax.rsqrt(lax.optimization_barrier(jnp.mean(hidden * hidden, axis=-1, keepdims=True)) + 1e-06) * norm_gain).astype(jnp.bfloat16)
    projected = jnp.dot(normed.reshape(-1, D), in_weight, preferred_element_type=jnp.float32).astype(jnp.bfloat16).reshape(GRID_ROW_COUNT, GRID_COLUMN_COUNT, 2 * E)
    pre_conv = projected[..., :E]
    gating_share = projected[..., E:]
    padded = jnp.pad(pre_conv, ((1, 1), (1, 1), (0, 0)))
    conv_sum = jnp.zeros((GRID_ROW_COUNT, GRID_COLUMN_COUNT, E), jnp.float32)
    for offset_row in range(3):
        for offset_col in range(3):
            conv_sum = conv_sum + padded[offset_row:offset_row + GRID_ROW_COUNT, offset_col:offset_col + GRID_COLUMN_COUNT].astype(jnp.float32) * conv_weight[3 * offset_row + offset_col]
    mixed_x = jax.nn.silu(conv_sum).astype(jnp.bfloat16)
    flat_x = mixed_x.reshape(-1, E)
    step_size = jax.nn.softplus(jnp.dot(flat_x, dt_weight, preferred_element_type=jnp.float32).reshape(GRID_ROW_COUNT, GRID_COLUMN_COUNT, 4, HEADS) + dt_bias)
    rates_all = jnp.concatenate([row_rate / (16.0 * GRID_COLUMN_COUNT), col_rate / (16.0 * GRID_ROW_COUNT)], 0)
    log_decay = -step_size * rates_all - horizon[:, :, None, None]
    signal = mixed_x.reshape(GRID_ROW_COUNT, GRID_COLUMN_COUNT, HEADS, HEAD_DIM)
    total = jnp.zeros((GRID_ROW_COUNT, GRID_COLUMN_COUNT, E), jnp.float32)
    for direction in range(4):
        coef_pair = jnp.dot(flat_x, bc_weight[:, direction * 2 * STATE:(direction + 1) * 2 * STATE], preferred_element_type=jnp.float32).astype(jnp.bfloat16).reshape(GRID_ROW_COUNT, GRID_COLUMN_COUNT, 2 * STATE)
        along_columns = direction >= 2
        backward = direction % 2 == 1
        signal_l = orient(signal, along_columns, backward)
        in_l = orient(coef_pair[..., :STATE], along_columns, backward)
        out_l = orient(coef_pair[..., STATE:], along_columns, backward)
        step_l = orient(step_size[:, :, direction], along_columns, backward)
        decay_l = orient(log_decay[:, :, direction], along_columns, backward)
        zero_states = jnp.zeros((signal_l.shape[0], HEADS, HEAD_DIM, STATE), jnp.float32)
        outputs = line_scan(signal_l, in_l, out_l, step_l, decay_l, zero_states)[0]
        total = total + restore(outputs, along_columns, backward)
    gated = (total * lax.rsqrt(lax.optimization_barrier(jnp.mean(total * total, axis=-1, keepdims=True)) + 1e-05) * out_gain * jax.nn.silu(gating_share.astype(jnp.float32))).astype(jnp.bfloat16)
    branch = jnp.dot(gated.reshape(-1, E), out_weight, preferred_element_type=jnp.float32).reshape(GRID_ROW_COUNT, GRID_COLUMN_COUNT, D)
    return (hidden + branch).astype(jnp.bfloat16)
```

```python
import functools

import jax
import jax.numpy as jnp
from jax import lax
from jax.experimental import pallas as pl
from jax.experimental.pallas import tpu as pltpu
from jax.sharding import PartitionSpec as P

MESH = pl.DeviceIdType.MESH
F32 = jnp.float32
BF16 = jnp.bfloat16


def exact_dot(a, b):
    return jnp.dot(a, b, preferred_element_type=F32, precision=lax.Precision.HIGHEST)


def dot(a, b):
    return jnp.dot(a.astype(BF16), b.astype(BF16), preferred_element_type=F32)


def dot_t(a, b):
    return lax.dot_general(
        a.astype(BF16), b.astype(BF16), (((1,), (1,)), ((), ())), preferred_element_type=F32
    )


def silu(v):
    return v / (1.0 + jnp.exp(-v))


def softplus(v):
    return jnp.maximum(v, 0.0) + jnp.log1p(jnp.exp(-jnp.abs(v)))


def kernel(
    n_row,
    n_col,
    latent_ref,
    logs_ref,
    cond_ref,
    trace_ref,
    norm_gain_ref,
    in_ref,
    conv_ref,
    bc_ref,
    dt_ref,
    dt_bias_ref,
    row_rate_ref,
    col_rate_ref,
    horizon_ref,
    out_gain_ref,
    out_weight_ref,
    out_ref,
    lat_f,
    logs_f,
    logs_all,
    logs_flat,
    picks,
    picks_side,
    edge_out,
    edge_line,
    edge_side,
    hz_row,
    hz_col,
    strip_row,
    strip_col,
    logs_send,
    logs_recv,
    edge_send,
    edge_recv,
    hz_send_r,
    hz_recv_r,
    hz_send_c,
    hz_recv_c,
    mix_send_r,
    mix_recv_r,
    mix_send_c,
    mix_recv_c,
):
    rows, cols, width = latent_ref.shape
    cells = rows * cols
    count = n_row * n_col
    inner = in_ref.shape[1] // 2
    heads = dt_bias_ref.shape[1]
    head_dim = inner // heads
    state = bc_ref.shape[1] // 8
    lanes = 4 * heads
    r = lax.axis_index("row")
    c = lax.axis_index("col")
    me = r * n_col + c
    n_token = logs_all.shape[0] * logs_all.shape[1]
    up, down = lax.rem(r + n_row - 1, n_row), lax.rem(r + 1, n_row)
    left, right = lax.rem(c + n_col - 1, n_col), lax.rem(c + 1, n_col)

    barrier = pltpu.get_barrier_semaphore()

    def greet(o, carry):
        d = lax.rem(me + o, count)
        pl.semaphore_signal(
            barrier, inc=1, device_id=(d // n_col, lax.rem(d, n_col)), device_id_type=MESH
        )
        return carry

    lax.fori_loop(1, count, greet, 0)

    lat = latent_ref[...].astype(F32)
    lat_f[...] = lat
    edge_out[0] = lat_f[:, 0, :]
    edge_out[1] = lat_f[:, cols - 1, :]
    logs_f[...] = logs_ref[...].astype(F32)
    logs_all[me] = logs_f[...]
    sub = lax.broadcasted_iota(jnp.int32, (cols, n_token), 0)
    lane = lax.broadcasted_iota(jnp.int32, (cols, n_token), 1)
    want = jnp.zeros((cols, n_token), jnp.int32)
    for j in range(cols):
        want = jnp.where(sub == j, trace_ref[j], want)
    picks[...] = (want == lane).astype(F32)
    hz_row[c] = horizon_ref[...]
    hz_col[r] = horizon_ref[...]

    pl.semaphore_wait(barrier, count - 1)

    def logs_copy(o):
        d = lax.rem(me + o, count)
        return pltpu.make_async_remote_copy(
            src_ref=logs_f,
            dst_ref=logs_all.at[me],
            send_sem=logs_send.at[o],
            recv_sem=logs_recv.at[o],
            device_id=(d // n_col, lax.rem(d, n_col)),
            device_id_type=MESH,
        )

    def start_logs(o, carry):
        logs_copy(o).start()
        return carry

    lax.fori_loop(1, count, start_logs, 0)

    last = rows - 1
    edges = []
    for src, dst, to in (
        (picks, picks_side.at[0], (r, right)),
        (picks, picks_side.at[1], (r, left)),
        (edge_out.at[1], edge_side.at[0], (r, right)),
        (edge_out.at[0], edge_side.at[1], (r, left)),
        (lat_f.at[last], edge_line.at[0], (down, c)),
        (lat_f.at[last], edge_line.at[1], (down, right)),
        (lat_f.at[last], edge_line.at[2], (down, left)),
        (lat_f.at[0], edge_line.at[3], (up, c)),
        (lat_f.at[0], edge_line.at[4], (up, right)),
        (lat_f.at[0], edge_line.at[5], (up, left)),
    ):
        k = len(edges)
        edges.append(
            pltpu.make_async_remote_copy(
                src_ref=src,
                dst_ref=dst,
                send_sem=edge_send.at[k],
                recv_sem=edge_recv.at[k],
                device_id=to,
                device_id_type=MESH,
            )
        )
        edges[-1].start()

    def fan(buffer_r, buffer_c, send_r, recv_r, send_c, recv_c):
        copies = []
        for o in range(1, n_col):
            copies.append(
                pltpu.make_async_remote_copy(
                    src_ref=buffer_r.at[c],
                    dst_ref=buffer_r.at[c],
                    send_sem=send_r.at[o],
                    recv_sem=recv_r.at[o],
                    device_id=(r, lax.rem(c + o, n_col)),
                    device_id_type=MESH,
                )
            )
        for o in range(1, n_row):
            copies.append(
                pltpu.make_async_remote_copy(
                    src_ref=buffer_c.at[r],
                    dst_ref=buffer_c.at[r],
                    send_sem=send_c.at[o],
                    recv_sem=recv_c.at[o],
                    device_id=(lax.rem(r + o, n_row), c),
                    device_id_type=MESH,
                )
            )
        for copy in copies:
            copy.start()
        return copies

    hz_copies = fan(hz_row, hz_col, hz_send_r, hz_recv_r, hz_send_c, hz_recv_c)

    head_of = lax.broadcasted_iota(jnp.int32, (heads, lanes), 1)
    spread = (
        lax.rem(head_of, heads) == lax.broadcasted_iota(jnp.int32, (heads, lanes), 0)
    ).astype(F32)

    def lane_row(table, first):
        wide = exact_dot(table, spread)
        kind = lax.broadcasted_iota(jnp.int32, wide.shape, 1) // heads
        own = lax.broadcasted_iota(jnp.int32, wide.shape, 0) + first
        return jnp.sum(jnp.where(kind == own, wide, 0.0), axis=0, keepdims=True)

    bias = lane_row(dt_bias_ref[...], 0)
    rates = lane_row(row_rate_ref[...] / (16.0 * cols * n_col), 0) + lane_row(
        col_rate_ref[...] / (16.0 * rows * n_row), 2
    )
    lane_dir = lax.broadcasted_iota(jnp.int32, (cells, lanes), 1) // heads
    ex_lane = lax.broadcasted_iota(jnp.int32, (lanes, inner), 0)
    ex_head = lax.broadcasted_iota(jnp.int32, (lanes, inner), 1) // head_dim
    expand = [(ex_lane == ex_head + k * heads).astype(BF16) for k in range(4)]

    cell_t = lax.broadcasted_iota(jnp.int32, (cells, cells), 0)
    cell_s = lax.broadcasted_iota(jnp.int32, (cells, cells), 1)
    ti, tj = cell_t // cols, lax.rem(cell_t, cols)
    si, sj = cell_s // cols, lax.rem(cell_s, cols)

    n_src = cells + 6 * cols + 2 * rows
    src_id = lax.broadcasted_iota(jnp.int32, (cells, n_src), 1)
    cell_id = lax.broadcasted_iota(jnp.int32, (cells, 1), 0)
    ci, cj = cell_id // cols, lax.rem(cell_id, cols)
    shifts = []
    for a in range(3):
        for b in range(3):
            pi, pj = ci + a - 1, cj + b - 1
            row_in = (pi >= 0) & (pi < rows)
            where_from = pi * cols + pj
            line_base = jnp.where(pi < 0, cells, cells + 3 * cols)
            line_from = line_base + jnp.where(
                pj < 0, 2 * cols - 1, jnp.where(pj >= cols, 2 * cols, pj)
            )
            side_from = cells + 6 * cols + pi + jnp.where(pj < 0, 0, rows)
            source = jnp.where(
                row_in, jnp.where((pj >= 0) & (pj < cols), where_from, side_from), line_from
            )
            gi, gj = r * rows + pi, c * cols + pj
            inside = (gi >= 0) & (gi < n_row * rows) & (gj >= 0) & (gj < n_col * cols)
            source = jnp.where(inside, source, -1)
            shifts.append((src_id == source).astype(BF16))

    def wait_logs(o, carry):
        logs_copy(o).wait()
        return carry

    lax.fori_loop(1, count, wait_logs, 0)
    per = logs_all.shape[1]
    for k in range(logs_all.shape[0]):
        logs_flat[pl.ds(k * per, per), :] = logs_all[k]
    tokens = silu(dot(logs_flat[...], cond_ref[...])).astype(BF16)

    for edge in edges:
        edge.wait()
    own_tokens = dot(picks[...], tokens)
    left_tokens = dot(picks_side[0], tokens)
    right_tokens = dot(picks_side[1], tokens)

    hidden_own = (lat_f[...] + own_tokens[None]).reshape(cells, width)
    left_token = left_tokens[cols - 1 : cols]
    right_token = right_tokens[0:1]
    hidden = jnp.concatenate(
        [
            hidden_own,
            edge_line[0] + own_tokens,
            edge_line[1] + left_tokens,
            edge_line[2] + right_tokens,
            edge_line[3] + own_tokens,
            edge_line[4] + left_tokens,
            edge_line[5] + right_tokens,
            edge_side[0] + left_token,
            edge_side[1] + right_token,
        ],
        axis=0,
    )
    normed = (
        hidden
        * lax.rsqrt(jnp.mean(hidden * hidden, axis=-1, keepdims=True) + 1e-06)
        * norm_gain_ref[...]
    ).astype(BF16)
    pre_conv = dot(normed, in_ref[:, :inner]).astype(BF16)
    gate_part = dot(normed[:cells], in_ref[:, inner:]).astype(BF16)
    conv_sum = jnp.zeros((cells, inner), F32)
    for k in range(9):
        conv_sum = conv_sum + dot(shifts[k], pre_conv) * conv_ref[k : k + 1, :]
    mixed = silu(conv_sum).astype(BF16)
    strip_row[c] = mixed
    strip_col[r] = mixed
    mix_copies = fan(strip_row, strip_col, mix_send_r, mix_recv_r, mix_send_c, mix_recv_c)

    mixed_f = mixed.astype(F32)
    coefs = dot(mixed, bc_ref[...]).astype(BF16)
    in_coef = [coefs[:, 2 * k * state : (2 * k + 1) * state] for k in range(4)]
    out_coef = [coefs[:, (2 * k + 1) * state : (2 * k + 2) * state] for k in range(4)]

    def spread_horizon(tile):
        pick = (
            lax.broadcasted_iota(jnp.int32, (cells, rows), 0) // cols
            == lax.broadcasted_iota(jnp.int32, (cells, rows), 1)
        ).astype(F32)
        wide = exact_dot(pick, tile)
        column = lax.rem(lax.broadcasted_iota(jnp.int32, (cells, cols), 0), cols)
        keep = column == lax.broadcasted_iota(jnp.int32, (cells, cols), 1)
        return jnp.sum(jnp.where(keep, wide, 0.0), axis=1, keepdims=True)

    def steps_of(x, marks):
        step = softplus(dot(x, dt_ref[...]) + bias)
        return step, -step * rates - marks

    step, decay = steps_of(mixed, spread_horizon(horizon_ref[...]))
    total = jnp.zeros((cells, inner), F32)
    entry = []
    for k in range(4):
        if k < 2:
            same, pt, ps, length = ti == si, tj, sj, cols
        else:
            same, pt, ps, length = tj == sj, ti, si, rows
        if k % 2 == 1:
            pt, ps = length - 1 - pt, length - 1 - ps
        scores = dot_t(out_coef[k], in_coef[k])
        total = total + dot(
            jnp.where(cell_t == cell_s, scores, 0.0), mixed_f * dot(step, expand[k])
        )
        half = length // 2
        while half >= 1:
            bt, bs = pt // half, ps // half
            late = lax.rem(bt, 2) == 1
            reach = same & (bt == bs) & ((late & (ps <= pt)) | (~late & (ps > pt)))
            factor = jnp.exp(exact_dot(reach.astype(F32), decay))
            pair = same & (bt == bs + 1) & late
            total = total + dot(factor, expand[k]) * dot(
                jnp.where(pair, scores, 0.0), mixed_f * dot(factor * step, expand[k])
            )
            half //= 2
        reach = (same & (ps <= pt)).astype(F32)
        entry.append(dot(jnp.exp(exact_dot(reach, decay)), expand[k]))

    for copy in hz_copies:
        copy.wait()
    marks_row = [spread_horizon(hz_row[q]) for q in range(n_col)]
    marks_col = [spread_horizon(hz_col[q]) for q in range(n_row)]
    for copy in mix_copies:
        copy.wait()

    for first, strip, marks, place, n, same, later in (
        (0, strip_row, marks_row, c, n_col, ti == si, sj - tj),
        (2, strip_col, marks_col, r, n_row, tj == sj, si - ti),
    ):
        after = (same & (later > 0)).astype(F32)
        before = (same & (later < 0)).astype(F32)
        whole = same.astype(F32)
        xs, steps, sums_f, sums_b, totals = [], [], [], [], []
        for q in range(n):
            x = strip[q]
            step, decay = steps_of(x, marks[q])
            xs.append(x)
            steps.append(step)
            sums_f.append(exact_dot(after, decay))
            sums_b.append(exact_dot(before, decay))
            totals.append(exact_dot(whole, decay))
        carry = jnp.zeros((cells, lanes), F32)
        for q in reversed(range(n)):
            sums_f[q] = sums_f[q] + carry
            carry = carry + jnp.where(q < place, totals[q], 0.0)
        carry = jnp.zeros((cells, lanes), F32)
        for q in range(n):
            sums_b[q] = sums_b[q] + carry
            carry = carry + jnp.where(q > place, totals[q], 0.0)
        both = expand[first] + expand[first + 1]
        weight_f = bc_ref[:, 2 * first * state : (2 * first + 1) * state]
        weight_b = bc_ref[:, (2 * first + 2) * state : (2 * first + 3) * state]
        for q in range(n):
            ahead = q < place
            use = ((lane_dir == first) & ahead) | ((lane_dir == first + 1) & (q > place))
            sums = jnp.where(lane_dir == first, sums_f[q], sums_b[q])
            gain = jnp.where(use, steps[q] * jnp.exp(sums), 0.0)
            driven = xs[q].astype(F32) * dot(gain, both)
            coef = dot(xs[q], jnp.where(ahead, weight_f, weight_b))
            reader = jnp.where(ahead, out_coef[first], out_coef[first + 1])
            scores = jnp.where(same, dot_t(reader, coef), 0.0)
            total = total + jnp.where(ahead, entry[first], entry[first + 1]) * dot(scores, driven)

    gated = (
        total
        * lax.rsqrt(jnp.mean(total * total, axis=-1, keepdims=True) + 1e-05)
        * out_gain_ref[...]
        * silu(gate_part.astype(F32))
    ).astype(BF16)
    result = hidden_own + dot(gated, out_weight_ref[...])
    out_ref[...] = result.reshape(rows, cols, width).astype(BF16)


def per_device(n_row, n_col, *args):
    (
        latent,
        logs,
        cond,
        trace,
        norm_gain,
        in_weight,
        conv,
        bc,
        dt,
        dt_bias,
        row_rate,
        col_rate,
        horizon,
        out_gain,
        out_weight,
    ) = args
    rows, cols, width = latent.shape
    inner = in_weight.shape[1] // 2
    cells = rows * cols
    count = n_row * n_col
    per = logs.shape[0]
    vmem = pl.BlockSpec(memory_space=pltpu.VMEM)
    specs = [vmem] * 15
    specs[3] = pl.BlockSpec(memory_space=pltpu.SMEM)
    dma = pltpu.SemaphoreType.DMA
    return pl.pallas_call(
        functools.partial(kernel, n_row, n_col),
        out_shape=jax.ShapeDtypeStruct((rows, cols, width), BF16),
        in_specs=specs,
        out_specs=vmem,
        scratch_shapes=[
            pltpu.VMEM((rows, cols, width), F32),
            pltpu.VMEM((per, width), F32),
            pltpu.VMEM((count, per, width), F32),
            pltpu.VMEM((count * per, width), F32),
            pltpu.VMEM((cols, count * per), F32),
            pltpu.VMEM((2, cols, count * per), F32),
            pltpu.VMEM((2, rows, width), F32),
            pltpu.VMEM((6, cols, width), F32),
            pltpu.VMEM((2, rows, width), F32),
            pltpu.VMEM((n_col, rows, cols), F32),
            pltpu.VMEM((n_row, rows, cols), F32),
            pltpu.VMEM((n_col, cells, inner), BF16),
            pltpu.VMEM((n_row, cells, inner), BF16),
            dma((count,)),
            dma((count,)),
            dma((10,)),
            dma((10,)),
            dma((n_col,)),
            dma((n_col,)),
            dma((n_row,)),
            dma((n_row,)),
            dma((n_col,)),
            dma((n_col,)),
            dma((n_row,)),
            dma((n_row,)),
        ],
        compiler_params=pltpu.CompilerParams(
            collective_id=0, has_side_effects=True, vmem_limit_bytes=48 * 1024 * 1024
        ),
    )(
        latent,
        logs,
        cond,
        trace,
        norm_gain.reshape(1, width),
        in_weight,
        conv,
        bc,
        dt,
        dt_bias,
        row_rate,
        col_rate,
        horizon,
        out_gain.reshape(1, inner),
        out_weight,
    )


def solution(mesh):
    placed = (
        P("row", "col", None),
        P(("row", "col"), None),
        P(),
        P("col"),
        P(),
        P(),
        P(),
        P(),
        P(),
        P(),
        P(),
        P(),
        P("row", "col"),
        P(),
        P(),
    )
    return jax.shard_map(
        functools.partial(per_device, mesh.shape["row"], mesh.shape["col"]),
        mesh=mesh,
        in_specs=placed,
        out_specs=P("row", "col", None),
        check_vma=False,
    )
```

```python
import functools

import jax
import jax.numpy as jnp
from jax import lax
from jax.experimental import pallas as pl
from jax.experimental.pallas import tpu as pltpu
from jax.sharding import PartitionSpec as P

MESH = pl.DeviceIdType.MESH
F32 = jnp.float32
BF16 = jnp.bfloat16


def exact_dot(a, b):
    return jnp.dot(a, b, preferred_element_type=F32, precision=lax.Precision.HIGHEST)


def dot(a, b):
    return jnp.dot(a.astype(BF16), b.astype(BF16), preferred_element_type=F32)


def dot_t(a, b):
    return lax.dot_general(
        a.astype(BF16), b.astype(BF16), (((1,), (1,)), ((), ())), preferred_element_type=F32
    )


def dot_first(a, b):
    return lax.dot_general(
        a.astype(BF16), b.astype(BF16), (((0,), (0,)), ((), ())), preferred_element_type=F32
    )


def split_dot(a, ones):
    high = a.astype(BF16)
    low = (a - high.astype(F32)).astype(BF16)
    both = jnp.dot(jnp.concatenate([high, low], axis=0), ones, preferred_element_type=F32)
    return both[: a.shape[0]] + both[a.shape[0] :]


def silu(v):
    return v / (1.0 + jnp.exp(-v))


def softplus(v):
    return jnp.maximum(v, 0.0) + jnp.log1p(jnp.exp(-jnp.abs(v)))


def kernel(
    n_row,
    n_col,
    latent_ref,
    logs_ref,
    cond_hbm,
    trace_ref,
    norm_gain_ref,
    in_hbm,
    conv_ref,
    bc_hbm,
    dt_ref,
    dt_bias_ref,
    row_rate_ref,
    col_rate_ref,
    horizon_ref,
    out_gain_ref,
    out_weight_hbm,
    out_ref,
    cond_ref,
    in_ref,
    bc_ref,
    out_weight_ref,
    weight_sem,
    shifts,
    lat_f,
    logs_f,
    logs_all,
    logs_flat,
    picks,
    picks_side,
    edge_out,
    edge_line,
    edge_side,
    hz_row,
    hz_col,
    strip_row,
    strip_col,
    logs_send,
    logs_recv,
    edge_send,
    edge_recv,
    hz_send_r,
    hz_recv_r,
    hz_send_c,
    hz_recv_c,
    mix_send_r,
    mix_recv_r,
    pass_send,
    pass_recv,
    mix_send_c,
    mix_recv_c,
):
    rows, cols, width = latent_ref.shape
    cells = rows * cols
    count = n_row * n_col
    inner = in_ref.shape[1] // 2
    heads = dt_bias_ref.shape[1]
    head_dim = inner // heads
    state = bc_ref.shape[1] // 8
    lanes = 4 * heads
    r = lax.axis_index("row")
    c = lax.axis_index("col")
    me = r * n_col + c
    n_token = logs_all.shape[0] * logs_all.shape[1]
    up, down = lax.rem(r + n_row - 1, n_row), lax.rem(r + 1, n_row)
    left, right = lax.rem(c + n_col - 1, n_col), lax.rem(c + 1, n_col)

    barrier = pltpu.get_barrier_semaphore()

    loads = [
        pltpu.make_async_copy(src, dst, weight_sem.at[k])
        for k, (src, dst) in enumerate(
            (
                (cond_hbm, cond_ref),
                (in_hbm, in_ref),
                (bc_hbm, bc_ref),
                (out_weight_hbm, out_weight_ref),
            )
        )
    ]
    for load in loads:
        load.start()

    def greet(o, carry):
        d = lax.rem(me + o, count)
        pl.semaphore_signal(
            barrier, inc=1, device_id=(d // n_col, lax.rem(d, n_col)), device_id_type=MESH
        )
        return carry

    lax.fori_loop(1, count, greet, 0)

    lat = latent_ref[...].astype(F32)
    lat_f[...] = lat
    edge_out[0] = lat_f[:, 0, :]
    edge_out[1] = lat_f[:, cols - 1, :]
    logs_f[...] = logs_ref[...].astype(F32)
    logs_all[me] = logs_f[...]
    sub = lax.broadcasted_iota(jnp.int32, (cols, n_token), 0)
    lane = lax.broadcasted_iota(jnp.int32, (cols, n_token), 1)
    want = jnp.zeros((cols, n_token), jnp.int32)
    for j in range(cols):
        want = jnp.where(sub == j, trace_ref[j], want)
    picks[...] = (want == lane).astype(F32)
    line_pick = (
        lax.broadcasted_iota(jnp.int32, (rows, cells), 1) // cols
        == lax.broadcasted_iota(jnp.int32, (rows, cells), 0)
    ).astype(F32)
    column_pick = lax.rem(
        lax.broadcasted_iota(jnp.int32, (cols, cells), 1), cols
    ) == lax.broadcasted_iota(jnp.int32, (cols, cells), 0)
    marks = jnp.sum(
        jnp.where(column_pick, exact_dot(horizon_ref[...], line_pick), 0.0), axis=0, keepdims=True
    )
    hz_row[c] = marks
    hz_col[r] = marks

    pl.semaphore_wait(barrier, count - 1)

    def logs_copy(o):
        d = lax.rem(me + o, count)
        return pltpu.make_async_remote_copy(
            src_ref=logs_f,
            dst_ref=logs_all.at[me],
            send_sem=logs_send.at[o],
            recv_sem=logs_recv.at[o],
            device_id=(d // n_col, lax.rem(d, n_col)),
            device_id_type=MESH,
        )

    def start_logs(o, carry):
        logs_copy(o).start()
        return carry

    lax.fori_loop(1, count, start_logs, 0)

    last = rows - 1
    edges = []
    for src, dst, to in (
        (picks, picks_side.at[0], (r, right)),
        (picks, picks_side.at[1], (r, left)),
        (edge_out.at[1], edge_side.at[0], (r, right)),
        (edge_out.at[0], edge_side.at[1], (r, left)),
        (lat_f.at[last], edge_line.at[0], (down, c)),
        (lat_f.at[last], edge_line.at[1], (down, right)),
        (lat_f.at[last], edge_line.at[2], (down, left)),
        (lat_f.at[0], edge_line.at[3], (up, c)),
        (lat_f.at[0], edge_line.at[4], (up, right)),
        (lat_f.at[0], edge_line.at[5], (up, left)),
    ):
        k = len(edges)
        edges.append(
            pltpu.make_async_remote_copy(
                src_ref=src,
                dst_ref=dst,
                send_sem=edge_send.at[k],
                recv_sem=edge_recv.at[k],
                device_id=to,
                device_id_type=MESH,
            )
        )
        edges[-1].start()

    def fan(buffer, place, n, axis, send, recv, step):
        copies = []
        for o in range(step, n, step):
            to = lax.rem(place + o, n)
            copies.append(
                pltpu.make_async_remote_copy(
                    src_ref=buffer.at[place],
                    dst_ref=buffer.at[place],
                    send_sem=send.at[o],
                    recv_sem=recv.at[o],
                    device_id=(to, c) if axis == 0 else (r, to),
                    device_id_type=MESH,
                )
            )
            copies[-1].start()
        return copies

    hz_copies = fan(hz_row, c, n_col, 1, hz_send_r, hz_recv_r, 1)
    hz_copies += fan(hz_col, r, n_row, 0, hz_send_c, hz_recv_c, 1)

    lane_head = lax.rem(lax.broadcasted_iota(jnp.int32, (lanes, heads), 0), heads)
    spread = (lane_head == lax.broadcasted_iota(jnp.int32, (lanes, heads), 1)).astype(F32)

    def lane_column(table, first):
        wide = lax.dot_general(
            spread,
            table,
            (((1,), (1,)), ((), ())),
            preferred_element_type=F32,
            precision=lax.Precision.HIGHEST,
        )
        kind = lax.broadcasted_iota(jnp.int32, wide.shape, 0) // heads
        own = lax.broadcasted_iota(jnp.int32, wide.shape, 1) + first
        return jnp.sum(jnp.where(kind == own, wide, 0.0), axis=1, keepdims=True)

    bias = lane_column(dt_bias_ref[...], 0)
    rates = lane_column(row_rate_ref[...] / (16.0 * cols * n_col), 0) + lane_column(
        col_rate_ref[...] / (16.0 * rows * n_row), 2
    )
    expand = (
        lax.broadcasted_iota(jnp.int32, (heads, inner), 0)
        == lax.broadcasted_iota(jnp.int32, (heads, inner), 1) // head_dim
    ).astype(BF16)

    cell_0 = lax.broadcasted_iota(jnp.int32, (cells, cells), 0)
    cell_1 = lax.broadcasted_iota(jnp.int32, (cells, cells), 1)
    i0, j0 = cell_0 // cols, lax.rem(cell_0, cols)
    i1, j1 = cell_1 // cols, lax.rem(cell_1, cols)

    n_src = cells + 6 * cols + 2 * rows
    src_id = lax.broadcasted_iota(jnp.int32, (cells, n_src), 1)
    cell_id = lax.broadcasted_iota(jnp.int32, (cells, 1), 0)
    ci, cj = cell_id // cols, lax.rem(cell_id, cols)
    for a in range(3):
        for b in range(3):
            pi, pj = ci + a - 1, cj + b - 1
            row_in = (pi >= 0) & (pi < rows)
            where_from = pi * cols + pj
            line_base = jnp.where(pi < 0, cells, cells + 3 * cols)
            line_from = line_base + jnp.where(
                pj < 0, 2 * cols - 1, jnp.where(pj >= cols, 2 * cols, pj)
            )
            side_from = cells + 6 * cols + pi + jnp.where(pj < 0, 0, rows)
            source = jnp.where(
                row_in, jnp.where((pj >= 0) & (pj < cols), where_from, side_from), line_from
            )
            gi, gj = r * rows + pi, c * cols + pj
            inside = (gi >= 0) & (gi < n_row * rows) & (gj >= 0) & (gj < n_col * cols)
            source = jnp.where(inside, source, -1)
            shifts[3 * a + b] = (src_id == source).astype(BF16)

    def wait_logs(o, carry):
        logs_copy(o).wait()
        return carry

    lax.fori_loop(1, count, wait_logs, 0)
    per = logs_all.shape[1]
    for k in range(logs_all.shape[0]):
        logs_flat[pl.ds(k * per, per), :] = logs_all[k]
    loads[0].wait()
    tokens = silu(dot(logs_flat[...], cond_ref[...])).astype(BF16)

    for edge in edges:
        edge.wait()
    own_tokens = dot(picks[...], tokens)
    left_tokens = dot(picks_side[0], tokens)
    right_tokens = dot(picks_side[1], tokens)

    hidden_own = (lat_f[...] + own_tokens[None]).reshape(cells, width)
    left_token = left_tokens[cols - 1 : cols]
    right_token = right_tokens[0:1]
    hidden = jnp.concatenate(
        [
            hidden_own,
            edge_line[0] + own_tokens,
            edge_line[1] + left_tokens,
            edge_line[2] + right_tokens,
            edge_line[3] + own_tokens,
            edge_line[4] + left_tokens,
            edge_line[5] + right_tokens,
            edge_side[0] + left_token,
            edge_side[1] + right_token,
        ],
        axis=0,
    )
    normed = (
        hidden
        * lax.rsqrt(jnp.mean(hidden * hidden, axis=-1, keepdims=True) + 1e-06)
        * norm_gain_ref[...]
    ).astype(BF16)
    loads[1].wait()
    pre_conv = dot(normed, in_ref[:, :inner]).astype(BF16)
    gate_part = dot(normed[:cells], in_ref[:, inner:]).astype(BF16)
    conv_sum = jnp.zeros((cells, inner), F32)
    for k in range(9):
        conv_sum = conv_sum + dot(shifts[k], pre_conv) * conv_ref[k : k + 1, :]
    mixed = silu(conv_sum).astype(BF16)
    strip_row[c] = mixed
    strip_col[r] = mixed
    sibling = c + 1 - 2 * lax.rem(c, 2)

    def to_sibling(e):
        place = lax.rem(c + n_col - 2 * e, n_col)
        return pltpu.make_async_remote_copy(
            src_ref=strip_row.at[place],
            dst_ref=strip_row.at[place],
            send_sem=pass_send.at[e],
            recv_sem=pass_recv.at[e],
            device_id=(r, sibling),
            device_id_type=MESH,
        )

    row_copies = fan(strip_row, c, n_col, 1, mix_send_r, mix_recv_r, 2)
    col_copies = fan(strip_col, r, n_row, 0, mix_send_c, mix_recv_c, 1)
    passed = [to_sibling(e) for e in range(n_col // 2)]
    passed[0].start()

    mixed_f = mixed.astype(F32)
    loads[2].wait()
    coefs = dot(mixed, bc_ref[...]).astype(BF16)
    in_coef = [coefs[:, 2 * k * state : (2 * k + 1) * state] for k in range(4)]
    out_coef = [coefs[:, (2 * k + 1) * state : (2 * k + 2) * state] for k in range(4)]

    def steps_of(x, marks, first, last):
        step = softplus(dot_t(dt_ref[first:last, :], x) + bias[first:last])
        return step, -step * rates[first:last] - marks

    step, decay = steps_of(mixed, marks, 0, lanes)
    total = jnp.zeros((cells, inner), F32)
    entry = []
    for k in range(4):
        if k < 2:
            same, p0, p1, length = i0 == i1, j0, j1, cols
        else:
            same, p0, p1, length = j0 == j1, i0, i1, rows
        if k % 2 == 1:
            p0, p1 = length - 1 - p0, length - 1 - p1
        halves = []
        while length > 1:
            length //= 2
            halves.append(length)
        reach = []
        for half in halves:
            block = (p0 // half) == (p1 // half)
            late = lax.rem(p1 // half, 2) == 1
            reach.append(same & block & ((late & (p0 <= p1)) | (~late & (p0 > p1))))
        reach.append(same & (p0 <= p1))
        sums = split_dot(
            decay[k * heads : (k + 1) * heads],
            jnp.concatenate([one.astype(BF16) for one in reach], axis=1),
        )
        own_step = step[k * heads : (k + 1) * heads]
        factor = jnp.exp(sums)
        wide = dot_first(
            jnp.concatenate(
                [factor.astype(BF16), (factor * jnp.tile(own_step, (1, len(reach)))).astype(BF16)]
                + [own_step.astype(BF16)],
                axis=1,
            ),
            expand,
        )
        wide = [wide[n * cells : (n + 1) * cells] for n in range(2 * len(reach) + 1)]
        scores = dot_t(out_coef[k], in_coef[k])
        total = total + dot(jnp.where(cell_0 == cell_1, scores, 0.0), mixed_f * wide[-1])
        for n, half in enumerate(halves):
            b0, b1 = p0 // half, p1 // half
            pair = same & (b0 == b1 + 1) & (lax.rem(b0, 2) == 1)
            total = total + wide[n] * dot(
                jnp.where(pair, scores, 0.0), mixed_f * wide[len(reach) + n]
            )
        entry.append(wide[len(halves)])

    def entering(first, strip, marks, place, n, same, later):
        after = (same & (later > 0)).astype(BF16)
        before = (same & (later < 0)).astype(BF16)
        whole = same.astype(BF16)
        x_all = strip[...].reshape(n * cells, inner)
        marks = jnp.concatenate([marks[q] for q in range(n)], axis=1)
        step, decay = steps_of(x_all, marks, first * heads, (first + 2) * heads)
        tile = [slice(q * cells, (q + 1) * cells) for q in range(n)]

        def stacked(part, ones):
            sums = split_dot(
                jnp.concatenate([part[:, tile[q]] for q in range(n)], axis=0),
                jnp.concatenate([ones, whole], axis=1),
            )
            sums = [sums[q * heads : (q + 1) * heads] for q in range(n)]
            return [one[:, :cells] for one in sums], [one[:, cells:] for one in sums]

        sums_f, totals_f = stacked(decay[:heads], after)
        sums_b, totals_b = stacked(decay[heads:], before)
        carry = jnp.zeros((heads, cells), F32)
        for q in reversed(range(n)):
            sums_f[q] = sums_f[q] + carry
            carry = carry + jnp.where(q < place, totals_f[q], 0.0)
        carry = jnp.zeros((heads, cells), F32)
        for q in range(n):
            sums_b[q] = sums_b[q] + carry
            carry = carry + jnp.where(q > place, totals_b[q], 0.0)
        gains = []
        for q in range(n):
            gain = jnp.where(q < place, step[:heads, tile[q]], step[heads:, tile[q]])
            gain = gain * jnp.exp(jnp.where(q < place, sums_f[q], sums_b[q]))
            gains.append(jnp.where(q == place, 0.0, gain))
        wide = dot_first(jnp.concatenate(gains, axis=1), expand)
        weight_f = bc_ref[:, 2 * first * state : (2 * first + 1) * state]
        weight_b = bc_ref[:, (2 * first + 2) * state : (2 * first + 3) * state]
        inflow = jnp.zeros((cells, inner), F32)
        for q in range(n):
            ahead = q < place
            x = x_all[tile[q]]
            driven = x.astype(F32) * wide[tile[q]]
            coef = dot(x, jnp.where(ahead, weight_f, weight_b))
            reader = jnp.where(ahead, out_coef[first], out_coef[first + 1])
            scores = jnp.where(same, dot_t(reader, coef), 0.0)
            inflow = inflow + jnp.where(ahead, entry[first], entry[first + 1]) * dot(
                scores, driven
            )
        return inflow

    for copy in hz_copies:
        copy.wait()
    for e, copy in enumerate(row_copies):
        copy.wait()
        passed[e + 1].start()
    for copy in col_copies:
        copy.wait()
    total = total + entering(2, strip_col, hz_col, r, n_row, j0 == j1, i0 - i1)
    for copy in passed:
        copy.wait()
    total = total + entering(0, strip_row, hz_row, c, n_col, i0 == i1, j0 - j1)

    gated = (
        total
        * lax.rsqrt(jnp.mean(total * total, axis=-1, keepdims=True) + 1e-05)
        * out_gain_ref[...]
        * silu(gate_part.astype(F32))
    ).astype(BF16)
    loads[3].wait()
    result = hidden_own + dot(gated, out_weight_ref[...])
    out_ref[...] = result.reshape(rows, cols, width).astype(BF16)


def per_device(n_row, n_col, *args):
    (
        latent,
        logs,
        cond,
        trace,
        norm_gain,
        in_weight,
        conv,
        bc,
        dt,
        dt_bias,
        row_rate,
        col_rate,
        horizon,
        out_gain,
        out_weight,
    ) = args
    rows, cols, width = latent.shape
    inner = in_weight.shape[1] // 2
    cells = rows * cols
    count = n_row * n_col
    per = logs.shape[0]
    vmem = pl.BlockSpec(memory_space=pltpu.VMEM)
    specs = [vmem] * 15
    specs[3] = pl.BlockSpec(memory_space=pltpu.SMEM)
    for k in (2, 5, 7, 14):
        specs[k] = pl.BlockSpec(memory_space=pltpu.HBM)
    dma = pltpu.SemaphoreType.DMA
    return pl.pallas_call(
        functools.partial(kernel, n_row, n_col),
        out_shape=jax.ShapeDtypeStruct((rows, cols, width), BF16),
        in_specs=specs,
        out_specs=vmem,
        scratch_shapes=[
            pltpu.VMEM(cond.shape, BF16),
            pltpu.VMEM(in_weight.shape, BF16),
            pltpu.VMEM(bc.shape, BF16),
            pltpu.VMEM(out_weight.shape, BF16),
            dma((4,)),
            pltpu.VMEM((9, cells, cells + 6 * cols + 2 * rows), BF16),
            pltpu.VMEM((rows, cols, width), F32),
            pltpu.VMEM((per, width), F32),
            pltpu.VMEM((count, per, width), F32),
            pltpu.VMEM((count * per, width), F32),
            pltpu.VMEM((cols, count * per), F32),
            pltpu.VMEM((2, cols, count * per), F32),
            pltpu.VMEM((2, rows, width), F32),
            pltpu.VMEM((6, cols, width), F32),
            pltpu.VMEM((2, rows, width), F32),
            pltpu.VMEM((n_col, 1, cells), F32),
            pltpu.VMEM((n_row, 1, cells), F32),
            pltpu.VMEM((n_col, cells, inner), BF16),
            pltpu.VMEM((n_row, cells, inner), BF16),
            dma((count,)),
            dma((count,)),
            dma((10,)),
            dma((10,)),
            dma((n_col,)),
            dma((n_col,)),
            dma((n_row,)),
            dma((n_row,)),
            dma((n_col,)),
            dma((n_col,)),
            dma((n_col // 2,)),
            dma((n_col // 2,)),
            dma((n_row,)),
            dma((n_row,)),
        ],
        compiler_params=pltpu.CompilerParams(
            collective_id=0, has_side_effects=True, vmem_limit_bytes=48 * 1024 * 1024
        ),
    )(
        latent,
        logs,
        cond,
        trace,
        norm_gain.reshape(1, width),
        in_weight,
        conv,
        bc,
        dt.T,
        dt_bias,
        row_rate,
        col_rate,
        horizon.T,
        out_gain.reshape(1, inner),
        out_weight,
    )


def solution(mesh):
    placed = (
        P("row", "col", None),
        P(("row", "col"), None),
        P(),
        P("col"),
        P(),
        P(),
        P(),
        P(),
        P(),
        P(),
        P(),
        P(),
        P("row", "col"),
        P(),
        P(),
    )
    return jax.shard_map(
        functools.partial(per_device, mesh.shape["row"], mesh.shape["col"]),
        mesh=mesh,
        in_specs=placed,
        out_specs=P("row", "col", None),
        check_vma=False,
    )
```

```python
import functools

import jax
import jax.numpy as jnp
from jax import lax
from jax.experimental import pallas as pl
from jax.experimental.pallas import tpu as pltpu
from jax.sharding import PartitionSpec as P

MESH = pl.DeviceIdType.MESH
F32 = jnp.float32
BF16 = jnp.bfloat16
VMEM_LIMIT = 64 * 1024 * 1024


def exact_dot(a, b):
    return jnp.dot(a, b, preferred_element_type=F32, precision=lax.Precision.HIGHEST)


def dot(a, b):
    return jnp.dot(a.astype(BF16), b.astype(BF16), preferred_element_type=F32)


def dot_t(a, b):
    return lax.dot_general(
        a.astype(BF16), b.astype(BF16), (((1,), (1,)), ((), ())), preferred_element_type=F32
    )


def dot_first(a, b):
    return lax.dot_general(
        a.astype(BF16), b.astype(BF16), (((0,), (0,)), ((), ())), preferred_element_type=F32
    )


def split_dot(a, ones):
    high = a.astype(BF16)
    low = (a - high.astype(F32)).astype(BF16)
    both = jnp.dot(jnp.concatenate([high, low], axis=0), ones, preferred_element_type=F32)
    return both[: a.shape[0]] + both[a.shape[0] :]


def silu(v):
    return v / (1.0 + jnp.exp(-v))


def softplus(v):
    return jnp.maximum(v, 0.0) + jnp.log1p(jnp.exp(-jnp.abs(v)))


def kernel(
    n_row,
    n_col,
    *refs,
):
    hbm, out_ref, own = refs[:15], refs[15], refs[16:31]
    (
        latent_ref,
        logs_ref,
        cond_ref,
        trace_ref,
        norm_gain_ref,
        in_ref,
        conv_ref,
        bc_ref,
        dt_ref,
        dt_bias_ref,
        row_rate_ref,
        col_rate_ref,
        horizon_ref,
        out_gain_ref,
        out_weight_ref,
    ) = own
    (
        load_sem,
        shifts,
        lat_f,
        logs_f,
        logs_all,
        logs_flat,
        picks,
        picks_side,
        edge_out,
        edge_line,
        edge_side,
        hz_row,
        hz_col,
        strip_row,
        strip_col,
        logs_send,
        logs_recv,
        edge_send,
        edge_recv,
        hz_send_r,
        hz_recv_r,
        hz_send_c,
        hz_recv_c,
        mix_send_r,
        mix_recv_r,
        pass_send,
        pass_recv,
        mix_send_c,
        mix_recv_c,
    ) = refs[31:]
    rows, cols, width = latent_ref.shape
    cells = rows * cols
    count = n_row * n_col
    inner = in_ref.shape[1] // 2
    heads = dt_bias_ref.shape[1]
    head_dim = inner // heads
    state = bc_ref.shape[1] // 8
    lanes = 4 * heads
    r = lax.axis_index("row")
    c = lax.axis_index("col")
    me = r * n_col + c
    n_token = logs_all.shape[0] * logs_all.shape[1]
    up, down = lax.rem(r + n_row - 1, n_row), lax.rem(r + 1, n_row)
    left, right = lax.rem(c + n_col - 1, n_col), lax.rem(c + 1, n_col)

    barrier = pltpu.get_barrier_semaphore()

    loads = [
        pltpu.make_async_copy(hbm[k], own[k], load_sem.at[k]) for k in range(len(hbm))
    ]
    for k in (0, 1, 12, 3, 2, 5, 4, 6, 7, 8, 9, 10, 11, 13, 14):
        loads[k].start()

    def greet(o, carry):
        d = lax.rem(me + o, count)
        pl.semaphore_signal(
            barrier, inc=1, device_id=(d // n_col, lax.rem(d, n_col)), device_id_type=MESH
        )
        return carry

    lax.fori_loop(1, count, greet, 0)

    for k in (0, 1, 3, 12):
        loads[k].wait()
    lat = latent_ref[...].astype(F32)
    lat_f[...] = lat
    edge_out[0] = lat_f[:, 0, :]
    edge_out[1] = lat_f[:, cols - 1, :]
    logs_f[...] = logs_ref[...].astype(F32)
    logs_all[me] = logs_f[...]
    sub = lax.broadcasted_iota(jnp.int32, (cols, n_token), 0)
    lane = lax.broadcasted_iota(jnp.int32, (cols, n_token), 1)
    want = jnp.zeros((cols, n_token), jnp.int32)
    for j in range(cols):
        want = jnp.where(sub == j, trace_ref[j], want)
    picks[...] = (want == lane).astype(F32)
    line_pick = (
        lax.broadcasted_iota(jnp.int32, (rows, cells), 1) // cols
        == lax.broadcasted_iota(jnp.int32, (rows, cells), 0)
    ).astype(F32)
    column_pick = lax.rem(
        lax.broadcasted_iota(jnp.int32, (cols, cells), 1), cols
    ) == lax.broadcasted_iota(jnp.int32, (cols, cells), 0)
    marks = jnp.sum(
        jnp.where(column_pick, exact_dot(horizon_ref[...], line_pick), 0.0), axis=0, keepdims=True
    )
    hz_row[c] = marks
    hz_col[r] = marks

    pl.semaphore_wait(barrier, count - 1)

    def logs_copy(o):
        d = lax.rem(me + o, count)
        return pltpu.make_async_remote_copy(
            src_ref=logs_f,
            dst_ref=logs_all.at[me],
            send_sem=logs_send.at[o],
            recv_sem=logs_recv.at[o],
            device_id=(d // n_col, lax.rem(d, n_col)),
            device_id_type=MESH,
        )

    def start_logs(o, carry):
        logs_copy(o).start()
        return carry

    lax.fori_loop(1, count, start_logs, 0)

    last = rows - 1
    edges = []
    for src, dst, to in (
        (picks, picks_side.at[0], (r, right)),
        (picks, picks_side.at[1], (r, left)),
        (edge_out.at[1], edge_side.at[0], (r, right)),
        (edge_out.at[0], edge_side.at[1], (r, left)),
        (lat_f.at[last], edge_line.at[0], (down, c)),
        (lat_f.at[last], edge_line.at[1], (down, right)),
        (lat_f.at[last], edge_line.at[2], (down, left)),
        (lat_f.at[0], edge_line.at[3], (up, c)),
        (lat_f.at[0], edge_line.at[4], (up, right)),
        (lat_f.at[0], edge_line.at[5], (up, left)),
    ):
        k = len(edges)
        edges.append(
            pltpu.make_async_remote_copy(
                src_ref=src,
                dst_ref=dst,
                send_sem=edge_send.at[k],
                recv_sem=edge_recv.at[k],
                device_id=to,
                device_id_type=MESH,
            )
        )
        edges[-1].start()

    def fan(buffer, place, n, axis, send, recv, step):
        copies = []
        for o in range(step, n, step):
            to = lax.rem(place + o, n)
            copies.append(
                pltpu.make_async_remote_copy(
                    src_ref=buffer.at[place],
                    dst_ref=buffer.at[place],
                    send_sem=send.at[o],
                    recv_sem=recv.at[o],
                    device_id=(to, c) if axis == 0 else (r, to),
                    device_id_type=MESH,
                )
            )
            copies[-1].start()
        return copies

    hz_copies = fan(hz_row, c, n_col, 1, hz_send_r, hz_recv_r, 1)
    hz_copies += fan(hz_col, r, n_row, 0, hz_send_c, hz_recv_c, 1)

    lane_head = lax.rem(lax.broadcasted_iota(jnp.int32, (lanes, heads), 0), heads)
    spread = (lane_head == lax.broadcasted_iota(jnp.int32, (lanes, heads), 1)).astype(F32)

    def lane_column(table, first):
        wide = lax.dot_general(
            spread,
            table,
            (((1,), (1,)), ((), ())),
            preferred_element_type=F32,
            precision=lax.Precision.HIGHEST,
        )
        kind = lax.broadcasted_iota(jnp.int32, wide.shape, 0) // heads
        own = lax.broadcasted_iota(jnp.int32, wide.shape, 1) + first
        return jnp.sum(jnp.where(kind == own, wide, 0.0), axis=1, keepdims=True)

    for k in (9, 10, 11):
        loads[k].wait()
    bias = lane_column(dt_bias_ref[...], 0)
    rates = lane_column(row_rate_ref[...] / (16.0 * cols * n_col), 0) + lane_column(
        col_rate_ref[...] / (16.0 * rows * n_row), 2
    )
    expand = (
        lax.broadcasted_iota(jnp.int32, (heads, inner), 0)
        == lax.broadcasted_iota(jnp.int32, (heads, inner), 1) // head_dim
    ).astype(BF16)

    cell_0 = lax.broadcasted_iota(jnp.int32, (cells, cells), 0)
    cell_1 = lax.broadcasted_iota(jnp.int32, (cells, cells), 1)
    i0, j0 = cell_0 // cols, lax.rem(cell_0, cols)
    i1, j1 = cell_1 // cols, lax.rem(cell_1, cols)

    n_src = cells + 6 * cols + 2 * rows
    src_id = lax.broadcasted_iota(jnp.int32, (cells, n_src), 1)
    cell_id = lax.broadcasted_iota(jnp.int32, (cells, 1), 0)
    ci, cj = cell_id // cols, lax.rem(cell_id, cols)
    for a in range(3):
        for b in range(3):
            pi, pj = ci + a - 1, cj + b - 1
            row_in = (pi >= 0) & (pi < rows)
            where_from = pi * cols + pj
            line_base = jnp.where(pi < 0, cells, cells + 3 * cols)
            line_from = line_base + jnp.where(
                pj < 0, 2 * cols - 1, jnp.where(pj >= cols, 2 * cols, pj)
            )
            side_from = cells + 6 * cols + pi + jnp.where(pj < 0, 0, rows)
            source = jnp.where(
                row_in, jnp.where((pj >= 0) & (pj < cols), where_from, side_from), line_from
            )
            gi, gj = r * rows + pi, c * cols + pj
            inside = (gi >= 0) & (gi < n_row * rows) & (gj >= 0) & (gj < n_col * cols)
            source = jnp.where(inside, source, -1)
            shifts[3 * a + b] = (src_id == source).astype(BF16)

    def wait_logs(o, carry):
        logs_copy(o).wait()
        return carry

    lax.fori_loop(1, count, wait_logs, 0)
    per = logs_all.shape[1]
    for k in range(logs_all.shape[0]):
        logs_flat[pl.ds(k * per, per), :] = logs_all[k]
    loads[2].wait()
    tokens = silu(dot(logs_flat[...], cond_ref[...])).astype(BF16)

    for edge in edges:
        edge.wait()
    own_tokens = dot(picks[...], tokens)
    left_tokens = dot(picks_side[0], tokens)
    right_tokens = dot(picks_side[1], tokens)

    hidden_own = (lat_f[...] + own_tokens[None]).reshape(cells, width)
    left_token = left_tokens[cols - 1 : cols]
    right_token = right_tokens[0:1]
    hidden = jnp.concatenate(
        [
            hidden_own,
            edge_line[0] + own_tokens,
            edge_line[1] + left_tokens,
            edge_line[2] + right_tokens,
            edge_line[3] + own_tokens,
            edge_line[4] + left_tokens,
            edge_line[5] + right_tokens,
            edge_side[0] + left_token,
            edge_side[1] + right_token,
        ],
        axis=0,
    )
    for k in (4, 5, 6):
        loads[k].wait()
    normed = (
        hidden
        * lax.rsqrt(jnp.mean(hidden * hidden, axis=-1, keepdims=True) + 1e-06)
        * norm_gain_ref[...]
    ).astype(BF16)
    pre_conv = dot(normed, in_ref[:, :inner]).astype(BF16)
    gate_part = dot(normed[:cells], in_ref[:, inner:]).astype(BF16)
    conv_sum = jnp.zeros((cells, inner), F32)
    for k in range(9):
        conv_sum = conv_sum + dot(shifts[k], pre_conv) * conv_ref[k : k + 1, :]
    mixed = silu(conv_sum).astype(BF16)
    strip_row[c] = mixed
    strip_col[r] = mixed
    sibling = c + 1 - 2 * lax.rem(c, 2)

    def to_sibling(e):
        place = lax.rem(c + n_col - 2 * e, n_col)
        return pltpu.make_async_remote_copy(
            src_ref=strip_row.at[place],
            dst_ref=strip_row.at[place],
            send_sem=pass_send.at[e],
            recv_sem=pass_recv.at[e],
            device_id=(r, sibling),
            device_id_type=MESH,
        )

    row_copies = fan(strip_row, c, n_col, 1, mix_send_r, mix_recv_r, 2)
    col_copies = fan(strip_col, r, n_row, 0, mix_send_c, mix_recv_c, 1)
    passed = [to_sibling(e) for e in range(n_col // 2)]
    passed[0].start()

    mixed_f = mixed.astype(F32)
    loads[7].wait()
    loads[8].wait()
    coefs = dot(mixed, bc_ref[...]).astype(BF16)
    in_coef = [coefs[:, 2 * k * state : (2 * k + 1) * state] for k in range(4)]
    out_coef = [coefs[:, (2 * k + 1) * state : (2 * k + 2) * state] for k in range(4)]

    def steps_of(x, marks, first, last):
        step = softplus(dot_t(dt_ref[first:last, :], x) + bias[first:last])
        return step, -step * rates[first:last] - marks

    step, decay = steps_of(mixed, marks, 0, lanes)
    total = jnp.zeros((cells, inner), F32)
    entry = []
    for k in range(4):
        if k < 2:
            same, p0, p1, length = i0 == i1, j0, j1, cols
        else:
            same, p0, p1, length = j0 == j1, i0, i1, rows
        if k % 2 == 1:
            p0, p1 = length - 1 - p0, length - 1 - p1
        halves = []
        while length > 1:
            length //= 2
            halves.append(length)
        reach = []
        for half in halves:
            block = (p0 // half) == (p1 // half)
            late = lax.rem(p1 // half, 2) == 1
            reach.append(same & block & ((late & (p0 <= p1)) | (~late & (p0 > p1))))
        reach.append(same & (p0 <= p1))
        sums = split_dot(
            decay[k * heads : (k + 1) * heads],
            jnp.concatenate([one.astype(BF16) for one in reach], axis=1),
        )
        own_step = step[k * heads : (k + 1) * heads]
        factor = jnp.exp(sums)
        wide = dot_first(
            jnp.concatenate(
                [factor.astype(BF16), (factor * jnp.tile(own_step, (1, len(reach)))).astype(BF16)]
                + [own_step.astype(BF16)],
                axis=1,
            ),
            expand,
        )
        wide = [wide[n * cells : (n + 1) * cells] for n in range(2 * len(reach) + 1)]
        scores = dot_t(out_coef[k], in_coef[k])
        total = total + dot(jnp.where(cell_0 == cell_1, scores, 0.0), mixed_f * wide[-1])
        for n, half in enumerate(halves):
            b0, b1 = p0 // half, p1 // half
            pair = same & (b0 == b1 + 1) & (lax.rem(b0, 2) == 1)
            total = total + wide[n] * dot(
                jnp.where(pair, scores, 0.0), mixed_f * wide[len(reach) + n]
            )
        entry.append(wide[len(halves)])

    def entering(first, strip, marks, place, n, same, later):
        after = (same & (later > 0)).astype(BF16)
        before = (same & (later < 0)).astype(BF16)
        whole = same.astype(BF16)
        x_all = strip[...].reshape(n * cells, inner)
        marks = jnp.concatenate([marks[q] for q in range(n)], axis=1)
        step, decay = steps_of(x_all, marks, first * heads, (first + 2) * heads)
        tile = [slice(q * cells, (q + 1) * cells) for q in range(n)]

        def stacked(part, ones):
            sums = split_dot(
                jnp.concatenate([part[:, tile[q]] for q in range(n)], axis=0),
                jnp.concatenate([ones, whole], axis=1),
            )
            sums = [sums[q * heads : (q + 1) * heads] for q in range(n)]
            return [one[:, :cells] for one in sums], [one[:, cells:] for one in sums]

        sums_f, totals_f = stacked(decay[:heads], after)
        sums_b, totals_b = stacked(decay[heads:], before)
        carry = jnp.zeros((heads, cells), F32)
        for q in reversed(range(n)):
            sums_f[q] = sums_f[q] + carry
            carry = carry + jnp.where(q < place, totals_f[q], 0.0)
        carry = jnp.zeros((heads, cells), F32)
        for q in range(n):
            sums_b[q] = sums_b[q] + carry
            carry = carry + jnp.where(q > place, totals_b[q], 0.0)
        gains = []
        for q in range(n):
            gain = jnp.where(q < place, step[:heads, tile[q]], step[heads:, tile[q]])
            gain = gain * jnp.exp(jnp.where(q < place, sums_f[q], sums_b[q]))
            gains.append(jnp.where(q == place, 0.0, gain))
        wide = dot_first(jnp.concatenate(gains, axis=1), expand)
        weight_f = bc_ref[:, 2 * first * state : (2 * first + 1) * state]
        weight_b = bc_ref[:, (2 * first + 2) * state : (2 * first + 3) * state]
        inflow = jnp.zeros((cells, inner), F32)
        for q in range(n):
            ahead = q < place
            x = x_all[tile[q]]
            driven = x.astype(F32) * wide[tile[q]]
            coef = dot(x, jnp.where(ahead, weight_f, weight_b))
            reader = jnp.where(ahead, out_coef[first], out_coef[first + 1])
            scores = jnp.where(same, dot_t(reader, coef), 0.0)
            inflow = inflow + jnp.where(ahead, entry[first], entry[first + 1]) * dot(
                scores, driven
            )
        return inflow

    for copy in hz_copies:
        copy.wait()
    for e, copy in enumerate(row_copies):
        copy.wait()
        passed[e + 1].start()
    for copy in col_copies:
        copy.wait()
    total = total + entering(2, strip_col, hz_col, r, n_row, j0 == j1, i0 - i1)
    for copy in passed:
        copy.wait()
    total = total + entering(0, strip_row, hz_row, c, n_col, i0 == i1, j0 - j1)

    loads[13].wait()
    loads[14].wait()
    gated = (
        total
        * lax.rsqrt(jnp.mean(total * total, axis=-1, keepdims=True) + 1e-05)
        * out_gain_ref[...]
        * silu(gate_part.astype(F32))
    ).astype(BF16)
    result = hidden_own + dot(gated, out_weight_ref[...])
    out_ref[...] = result.reshape(rows, cols, width).astype(BF16)


def per_device(n_row, n_col, *args):
    (
        latent,
        logs,
        cond,
        trace,
        norm_gain,
        in_weight,
        conv,
        bc,
        dt,
        dt_bias,
        row_rate,
        col_rate,
        horizon,
        out_gain,
        out_weight,
    ) = args
    rows, cols, width = latent.shape
    inner = in_weight.shape[1] // 2
    cells = rows * cols
    count = n_row * n_col
    per = logs.shape[0]
    vmem = pl.BlockSpec(memory_space=pltpu.VMEM)
    operands = (
        latent,
        logs,
        cond,
        trace,
        norm_gain.reshape(1, width),
        in_weight,
        conv,
        bc,
        dt.T,
        dt_bias,
        row_rate,
        col_rate,
        horizon.T,
        out_gain.reshape(1, inner),
        out_weight,
    )
    own = [pltpu.VMEM(one.shape, one.dtype) for one in operands]
    own[3] = pltpu.SMEM(trace.shape, trace.dtype)
    dma = pltpu.SemaphoreType.DMA
    return pl.pallas_call(
        functools.partial(kernel, n_row, n_col),
        out_shape=jax.ShapeDtypeStruct((rows, cols, width), BF16),
        in_specs=[pl.BlockSpec(memory_space=pltpu.HBM)] * len(operands),
        out_specs=vmem,
        scratch_shapes=own
        + [
            dma((len(operands),)),
            pltpu.VMEM((9, cells, cells + 6 * cols + 2 * rows), BF16),
            pltpu.VMEM((rows, cols, width), F32),
            pltpu.VMEM((per, width), F32),
            pltpu.VMEM((count, per, width), F32),
            pltpu.VMEM((count * per, width), F32),
            pltpu.VMEM((cols, count * per), F32),
            pltpu.VMEM((2, cols, count * per), F32),
            pltpu.VMEM((2, rows, width), F32),
            pltpu.VMEM((6, cols, width), F32),
            pltpu.VMEM((2, rows, width), F32),
            pltpu.VMEM((n_col, 1, cells), F32),
            pltpu.VMEM((n_row, 1, cells), F32),
            pltpu.VMEM((n_col, cells, inner), BF16),
            pltpu.VMEM((n_row, cells, inner), BF16),
            dma((count,)),
            dma((count,)),
            dma((10,)),
            dma((10,)),
            dma((n_col,)),
            dma((n_col,)),
            dma((n_row,)),
            dma((n_row,)),
            dma((n_col,)),
            dma((n_col,)),
            dma((n_col // 2,)),
            dma((n_col // 2,)),
            dma((n_row,)),
            dma((n_row,)),
        ],
        compiler_params=pltpu.CompilerParams(
            collective_id=0, has_side_effects=True, vmem_limit_bytes=VMEM_LIMIT
        ),
    )(*operands)


def solution(mesh):
    placed = (
        P("row", "col", None),
        P(("row", "col"), None),
        P(),
        P("col"),
        P(),
        P(),
        P(),
        P(),
        P(),
        P(),
        P(),
        P(),
        P("row", "col"),
        P(),
        P(),
    )
    return jax.shard_map(
        functools.partial(per_device, mesh.shape["row"], mesh.shape["col"]),
        mesh=mesh,
        in_specs=placed,
        out_specs=P("row", "col", None),
        check_vma=False,
    )
```

```python
import functools

import jax
import jax.numpy as jnp
from jax import lax
from jax.experimental import pallas as pl
from jax.experimental.pallas import tpu as pltpu
from jax.sharding import PartitionSpec as P

MESH = pl.DeviceIdType.MESH
F32 = jnp.float32
BF16 = jnp.bfloat16
VMEM_LIMIT = 64 * 1024 * 1024


def exact_dot(a, b):
    return jnp.dot(a, b, preferred_element_type=F32, precision=lax.Precision.HIGHEST)


def dot(a, b):
    return jnp.dot(a.astype(BF16), b.astype(BF16), preferred_element_type=F32)


def dot_t(a, b):
    return lax.dot_general(
        a.astype(BF16), b.astype(BF16), (((1,), (1,)), ((), ())), preferred_element_type=F32
    )


def dot_first(a, b):
    return lax.dot_general(
        a.astype(BF16), b.astype(BF16), (((0,), (0,)), ((), ())), preferred_element_type=F32
    )


def split_dot(a, ones):
    high = a.astype(BF16)
    low = (a - high.astype(F32)).astype(BF16)
    both = jnp.dot(jnp.concatenate([high, low], axis=0), ones, preferred_element_type=F32)
    return both[: a.shape[0]] + both[a.shape[0] :]


def silu(v):
    return v / (1.0 + jnp.exp(-v))


def softplus(v):
    return jnp.maximum(v, 0.0) + jnp.log1p(jnp.exp(-jnp.abs(v)))


def kernel(
    n_row,
    n_col,
    *refs,
):
    hbm, out_ref, own = refs[:15], refs[15], refs[16:31]
    (
        latent_ref,
        logs_ref,
        cond_ref,
        trace_ref,
        norm_gain_ref,
        in_ref,
        conv_ref,
        bc_ref,
        dt_ref,
        dt_bias_ref,
        row_rate_ref,
        col_rate_ref,
        horizon_ref,
        out_gain_ref,
        out_weight_ref,
    ) = own
    (
        load_sem,
        shifts,
        lat_f,
        logs_f,
        logs_all,
        logs_flat,
        picks,
        picks_side,
        edge_out,
        edge_line,
        edge_side,
        hz_row,
        hz_col,
        strip_row,
        strip_col,
        logs_send,
        logs_recv,
        edge_send,
        edge_recv,
        hz_send_r,
        hz_recv_r,
        hz_send_c,
        hz_recv_c,
        mix_send_r,
        mix_recv_r,
        pass_send,
        pass_recv,
        mix_send_c,
        mix_recv_c,
    ) = refs[31:]
    rows, cols, width = latent_ref.shape
    cells = rows * cols
    count = n_row * n_col
    inner = in_ref.shape[1] // 2
    heads = dt_bias_ref.shape[1]
    head_dim = inner // heads
    state = bc_ref.shape[1] // 8
    lanes = 4 * heads
    r = lax.axis_index("row")
    c = lax.axis_index("col")
    me = r * n_col + c
    n_token = logs_all.shape[0] * logs_all.shape[1]
    up, down = lax.rem(r + n_row - 1, n_row), lax.rem(r + 1, n_row)
    left, right = lax.rem(c + n_col - 1, n_col), lax.rem(c + 1, n_col)

    barrier = pltpu.get_barrier_semaphore()

    loads = [
        pltpu.make_async_copy(hbm[k], own[k], load_sem.at[k]) for k in range(len(hbm))
    ]
    for k in (0, 1, 12, 3, 2, 5, 4, 6, 7, 8, 9, 10, 11, 13, 14):
        loads[k].start()

    row_of = [lax.rem(r + o, n_row) for o in range(n_row)]
    col_of = [lax.rem(c + o, n_col) for o in range(n_col)]
    others = [(i, j) for i in range(n_row) for j in range(n_col) if i + j > 0]
    for i, j in others:
        pl.semaphore_signal(
            barrier, inc=1, device_id=(row_of[i], col_of[j]), device_id_type=MESH
        )

    for k in (0, 1, 3, 12):
        loads[k].wait()
    lat = latent_ref[...].astype(F32)
    lat_f[...] = lat
    edge_out[0] = lat_f[:, 0, :]
    edge_out[1] = lat_f[:, cols - 1, :]
    logs_f[...] = logs_ref[...].astype(F32)
    logs_all[me] = logs_f[...]
    sub = lax.broadcasted_iota(jnp.int32, (cols, n_token), 0)
    lane = lax.broadcasted_iota(jnp.int32, (cols, n_token), 1)
    want = jnp.zeros((cols, n_token), jnp.int32)
    for j in range(cols):
        want = jnp.where(sub == j, trace_ref[j], want)
    picks[...] = (want == lane).astype(F32)
    line_pick = (
        lax.broadcasted_iota(jnp.int32, (rows, cells), 1) // cols
        == lax.broadcasted_iota(jnp.int32, (rows, cells), 0)
    ).astype(F32)
    column_pick = lax.rem(
        lax.broadcasted_iota(jnp.int32, (cols, cells), 1), cols
    ) == lax.broadcasted_iota(jnp.int32, (cols, cells), 0)
    marks = jnp.sum(
        jnp.where(column_pick, exact_dot(horizon_ref[...], line_pick), 0.0), axis=0, keepdims=True
    )
    hz_row[c] = marks
    hz_col[r] = marks

    pl.semaphore_wait(barrier, count - 1)

    for i, j in others:
        pltpu.make_async_remote_copy(
            src_ref=logs_f,
            dst_ref=logs_all.at[me],
            send_sem=logs_send,
            recv_sem=logs_recv,
            device_id=(row_of[i], col_of[j]),
            device_id_type=MESH,
        ).start()

    last = rows - 1
    edges = []
    for src, dst, to in (
        (picks, picks_side.at[0], (r, right)),
        (picks, picks_side.at[1], (r, left)),
        (edge_out.at[1], edge_side.at[0], (r, right)),
        (edge_out.at[0], edge_side.at[1], (r, left)),
        (lat_f.at[last], edge_line.at[0], (down, c)),
        (lat_f.at[last], edge_line.at[1], (down, right)),
        (lat_f.at[last], edge_line.at[2], (down, left)),
        (lat_f.at[0], edge_line.at[3], (up, c)),
        (lat_f.at[0], edge_line.at[4], (up, right)),
        (lat_f.at[0], edge_line.at[5], (up, left)),
    ):
        k = len(edges)
        edges.append(
            pltpu.make_async_remote_copy(
                src_ref=src,
                dst_ref=dst,
                send_sem=edge_send.at[k],
                recv_sem=edge_recv.at[k],
                device_id=to,
                device_id_type=MESH,
            )
        )
        edges[-1].start()

    def fan(buffer, place, n, axis, send, recv, step):
        copies = []
        for o in range(step, n, step):
            to = lax.rem(place + o, n)
            copies.append(
                pltpu.make_async_remote_copy(
                    src_ref=buffer.at[place],
                    dst_ref=buffer.at[place],
                    send_sem=send.at[o],
                    recv_sem=recv.at[o],
                    device_id=(to, c) if axis == 0 else (r, to),
                    device_id_type=MESH,
                )
            )
            copies[-1].start()
        return copies

    hz_copies = fan(hz_row, c, n_col, 1, hz_send_r, hz_recv_r, 1)
    hz_copies += fan(hz_col, r, n_row, 0, hz_send_c, hz_recv_c, 1)

    lane_head = lax.rem(lax.broadcasted_iota(jnp.int32, (lanes, heads), 0), heads)
    spread = (lane_head == lax.broadcasted_iota(jnp.int32, (lanes, heads), 1)).astype(F32)

    def lane_column(table, first):
        wide = lax.dot_general(
            spread,
            table,
            (((1,), (1,)), ((), ())),
            preferred_element_type=F32,
            precision=lax.Precision.HIGHEST,
        )
        kind = lax.broadcasted_iota(jnp.int32, wide.shape, 0) // heads
        own = lax.broadcasted_iota(jnp.int32, wide.shape, 1) + first
        return jnp.sum(jnp.where(kind == own, wide, 0.0), axis=1, keepdims=True)

    for k in (9, 10, 11):
        loads[k].wait()
    bias = lane_column(dt_bias_ref[...], 0)
    rates = lane_column(row_rate_ref[...] / (16.0 * cols * n_col), 0) + lane_column(
        col_rate_ref[...] / (16.0 * rows * n_row), 2
    )
    expand = (
        lax.broadcasted_iota(jnp.int32, (heads, inner), 0)
        == lax.broadcasted_iota(jnp.int32, (heads, inner), 1) // head_dim
    ).astype(BF16)

    cell_0 = lax.broadcasted_iota(jnp.int32, (cells, cells), 0)
    cell_1 = lax.broadcasted_iota(jnp.int32, (cells, cells), 1)
    i0, j0 = cell_0 // cols, lax.rem(cell_0, cols)
    i1, j1 = cell_1 // cols, lax.rem(cell_1, cols)

    n_src = cells + 6 * cols + 2 * rows
    src_id = lax.broadcasted_iota(jnp.int32, (cells, n_src), 1)
    cell_id = lax.broadcasted_iota(jnp.int32, (cells, 1), 0)
    ci, cj = cell_id // cols, lax.rem(cell_id, cols)
    for a in range(3):
        for b in range(3):
            pi, pj = ci + a - 1, cj + b - 1
            row_in = (pi >= 0) & (pi < rows)
            where_from = pi * cols + pj
            line_base = jnp.where(pi < 0, cells, cells + 3 * cols)
            line_from = line_base + jnp.where(
                pj < 0, 2 * cols - 1, jnp.where(pj >= cols, 2 * cols, pj)
            )
            side_from = cells + 6 * cols + pi + jnp.where(pj < 0, 0, rows)
            source = jnp.where(
                row_in, jnp.where((pj >= 0) & (pj < cols), where_from, side_from), line_from
            )
            gi, gj = r * rows + pi, c * cols + pj
            inside = (gi >= 0) & (gi < n_row * rows) & (gj >= 0) & (gj < n_col * cols)
            source = jnp.where(inside, source, -1)
            shifts[3 * a + b] = (src_id == source).astype(BF16)

    def wait_for(part, sem):
        pltpu.make_async_copy(part, part, sem).wait()

    arrived = logs_all.at[pl.ds(0, count - 1)]
    wait_for(arrived, logs_recv)
    wait_for(arrived, logs_send)
    per = logs_all.shape[1]
    for k in range(logs_all.shape[0]):
        logs_flat[pl.ds(k * per, per), :] = logs_all[k]
    loads[2].wait()
    tokens = silu(dot(logs_flat[...], cond_ref[...])).astype(BF16)

    for edge in edges:
        edge.wait()
    own_tokens = dot(picks[...], tokens)
    left_tokens = dot(picks_side[0], tokens)
    right_tokens = dot(picks_side[1], tokens)

    hidden_own = (lat_f[...] + own_tokens[None]).reshape(cells, width)
    left_token = left_tokens[cols - 1 : cols]
    right_token = right_tokens[0:1]
    hidden = jnp.concatenate(
        [
            hidden_own,
            edge_line[0] + own_tokens,
            edge_line[1] + left_tokens,
            edge_line[2] + right_tokens,
            edge_line[3] + own_tokens,
            edge_line[4] + left_tokens,
            edge_line[5] + right_tokens,
            edge_side[0] + left_token,
            edge_side[1] + right_token,
        ],
        axis=0,
    )
    for k in (4, 5, 6):
        loads[k].wait()
    normed = (
        hidden
        * lax.rsqrt(jnp.mean(hidden * hidden, axis=-1, keepdims=True) + 1e-06)
        * norm_gain_ref[...]
    ).astype(BF16)
    pre_conv = dot(normed, in_ref[:, :inner]).astype(BF16)
    gate_part = dot(normed[:cells], in_ref[:, inner:]).astype(BF16)
    conv_sum = jnp.zeros((cells, inner), F32)
    for k in range(9):
        conv_sum = conv_sum + dot(shifts[k], pre_conv) * conv_ref[k : k + 1, :]
    mixed = silu(conv_sum).astype(BF16)
    strip_row[c] = mixed
    strip_col[r] = mixed
    sibling = c + 1 - 2 * lax.rem(c, 2)

    def to_sibling(e):
        place = lax.rem(c + n_col - 2 * e, n_col)
        return pltpu.make_async_remote_copy(
            src_ref=strip_row.at[place],
            dst_ref=strip_row.at[place],
            send_sem=pass_send.at[e],
            recv_sem=pass_recv.at[e],
            device_id=(r, sibling),
            device_id_type=MESH,
        )

    row_copies = fan(strip_row, c, n_col, 1, mix_send_r, mix_recv_r, 2)
    col_copies = fan(strip_col, r, n_row, 0, mix_send_c, mix_recv_c, 1)
    passed = [to_sibling(e) for e in range(n_col // 2)]
    passed[0].start()

    mixed_f = mixed.astype(F32)
    loads[7].wait()
    loads[8].wait()
    coefs = dot(mixed, bc_ref[...]).astype(BF16)
    in_coef = [coefs[:, 2 * k * state : (2 * k + 1) * state] for k in range(4)]
    out_coef = [coefs[:, (2 * k + 1) * state : (2 * k + 2) * state] for k in range(4)]

    def steps_of(x, marks, first, last):
        step = softplus(dot_t(dt_ref[first:last, :], x) + bias[first:last])
        return step, -step * rates[first:last] - marks

    step, decay = steps_of(mixed, marks, 0, lanes)
    total = jnp.zeros((cells, inner), F32)
    entry = []
    for k in range(4):
        if k < 2:
            same, p0, p1, length = i0 == i1, j0, j1, cols
        else:
            same, p0, p1, length = j0 == j1, i0, i1, rows
        if k % 2 == 1:
            p0, p1 = length - 1 - p0, length - 1 - p1
        halves = []
        while length > 1:
            length //= 2
            halves.append(length)
        reach = []
        for half in halves:
            block = (p0 // half) == (p1 // half)
            late = lax.rem(p1 // half, 2) == 1
            reach.append(same & block & ((late & (p0 <= p1)) | (~late & (p0 > p1))))
        reach.append(same & (p0 <= p1))
        sums = split_dot(
            decay[k * heads : (k + 1) * heads],
            jnp.concatenate([one.astype(BF16) for one in reach], axis=1),
        )
        own_step = step[k * heads : (k + 1) * heads]
        factor = jnp.exp(sums[:, : len(halves) * cells])
        wide = dot_first(
            jnp.concatenate(
                [factor, factor * jnp.tile(own_step, (1, len(halves))), own_step], axis=1
            ),
            expand,
        )
        wide = [wide[n * cells : (n + 1) * cells] for n in range(2 * len(halves) + 1)]
        scores = dot_t(out_coef[k], in_coef[k])
        total = total + dot(jnp.where(cell_0 == cell_1, scores, 0.0), mixed_f * wide[-1])
        for n, half in enumerate(halves):
            b0, b1 = p0 // half, p1 // half
            pair = same & (b0 == b1 + 1) & (lax.rem(b0, 2) == 1)
            total = total + wide[n] * dot(
                jnp.where(pair, scores, 0.0), mixed_f * wide[len(halves) + n]
            )
        entry.append(sums[:, len(halves) * cells :])

    def entering(first, strip, marks, place, tiles, same, later):
        after = (same & (later > 0)).astype(BF16)
        before = (same & (later < 0)).astype(BF16)
        whole = same.astype(BF16)
        n = len(tiles)
        xs = [strip[q] for q in tiles]
        marks = jnp.concatenate([marks[q] for q in tiles], axis=1)
        step, decay = steps_of(
            jnp.concatenate(xs, axis=0), marks, first * heads, (first + 2) * heads
        )
        tile = [slice(m * cells, (m + 1) * cells) for m in range(n)]

        def stacked(part, ones):
            sums = split_dot(
                jnp.concatenate([part[:, tile[m]] for m in range(n)], axis=0),
                jnp.concatenate([ones, whole], axis=1),
            )
            sums = [sums[m * heads : (m + 1) * heads] for m in range(n)]
            return [one[:, :cells] for one in sums], [one[:, cells:] for one in sums]

        sums_f, totals_f = stacked(decay[:heads], after)
        sums_b, totals_b = stacked(decay[heads:], before)
        gains = []
        for m, q in enumerate(tiles):
            gain = jnp.where(q < place, step[:heads, tile[m]], step[heads:, tile[m]])
            gains.append(gain * jnp.exp(jnp.where(q < place, sums_f[m], sums_b[m])))
        wide = dot_first(jnp.concatenate(gains, axis=1), expand)
        weight_f = bc_ref[:, 2 * first * state : (2 * first + 1) * state]
        weight_b = bc_ref[:, (2 * first + 2) * state : (2 * first + 3) * state]
        out = []
        for m, q in enumerate(tiles):
            ahead = q < place
            driven = xs[m].astype(F32) * wide[tile[m]]
            coef = dot(xs[m], jnp.where(ahead, weight_f, weight_b))
            reader = jnp.where(ahead, out_coef[first], out_coef[first + 1])
            scores = jnp.where(same, dot_t(reader, coef), 0.0)
            out.append((q, jnp.where(ahead, totals_f[m], totals_b[m]), dot(scores, driven)))
        return out

    def decayed(first, place, parts):
        exponents = []
        for q, _, _ in parts:
            exponent = jnp.where(q < place, entry[first], entry[first + 1])
            for other, between, _ in parts:
                inner_f = (q < other) & (other < place)
                inner_b = (q > other) & (other > place)
                exponent = exponent + jnp.where(inner_f | inner_b, between, 0.0)
            exponents.append(exponent)
        wide = dot_first(jnp.exp(jnp.concatenate(exponents, axis=1)), expand)
        inflow = jnp.zeros((cells, inner), F32)
        for m, (_, _, part) in enumerate(parts):
            inflow = inflow + wide[m * cells : (m + 1) * cells] * part
        return inflow

    for copy in hz_copies:
        copy.wait()
    for e, copy in enumerate(row_copies):
        copy.wait()
        passed[e + 1].start()
    for copy in col_copies:
        copy.wait()
    others_r = [lax.rem(r + n_row - o, n_row) for o in range(1, n_row)]
    total = total + decayed(
        2, r, entering(2, strip_col, hz_col, r, others_r, j0 == j1, i0 - i1)
    )
    passed[0].wait()
    near = [sibling] + [lax.rem(c + n_col - o, n_col) for o in range(2, n_col, 2)]
    far = [lax.rem(sibling + n_col - o, n_col) for o in range(2, n_col, 2)]
    parts = entering(0, strip_row, hz_row, c, near, i0 == i1, j0 - j1)
    for copy in passed[1:]:
        copy.wait()
    parts += entering(0, strip_row, hz_row, c, far, i0 == i1, j0 - j1)
    total = total + decayed(0, c, parts)

    loads[13].wait()
    loads[14].wait()
    gated = (
        total
        * lax.rsqrt(jnp.mean(total * total, axis=-1, keepdims=True) + 1e-05)
        * out_gain_ref[...]
        * silu(gate_part.astype(F32))
    ).astype(BF16)
    result = hidden_own + dot(gated, out_weight_ref[...])
    out_ref[...] = result.reshape(rows, cols, width).astype(BF16)


def per_device(n_row, n_col, *args):
    (
        latent,
        logs,
        cond,
        trace,
        norm_gain,
        in_weight,
        conv,
        bc,
        dt,
        dt_bias,
        row_rate,
        col_rate,
        horizon,
        out_gain,
        out_weight,
    ) = args
    rows, cols, width = latent.shape
    inner = in_weight.shape[1] // 2
    cells = rows * cols
    count = n_row * n_col
    per = logs.shape[0]
    vmem = pl.BlockSpec(memory_space=pltpu.VMEM)
    operands = (
        latent,
        logs,
        cond,
        trace,
        norm_gain.reshape(1, width),
        in_weight,
        conv,
        bc,
        dt.T,
        dt_bias,
        row_rate,
        col_rate,
        horizon.T,
        out_gain.reshape(1, inner),
        out_weight,
    )
    own = [pltpu.VMEM(one.shape, one.dtype) for one in operands]
    own[3] = pltpu.SMEM(trace.shape, trace.dtype)
    dma = pltpu.SemaphoreType.DMA
    return pl.pallas_call(
        functools.partial(kernel, n_row, n_col),
        out_shape=jax.ShapeDtypeStruct((rows, cols, width), BF16),
        in_specs=[pl.BlockSpec(memory_space=pltpu.HBM)] * len(operands),
        out_specs=vmem,
        scratch_shapes=own
        + [
            dma((len(operands),)),
            pltpu.VMEM((9, cells, cells + 6 * cols + 2 * rows), BF16),
            pltpu.VMEM((rows, cols, width), F32),
            pltpu.VMEM((per, width), F32),
            pltpu.VMEM((count, per, width), F32),
            pltpu.VMEM((count * per, width), F32),
            pltpu.VMEM((cols, count * per), F32),
            pltpu.VMEM((2, cols, count * per), F32),
            pltpu.VMEM((2, rows, width), F32),
            pltpu.VMEM((6, cols, width), F32),
            pltpu.VMEM((2, rows, width), F32),
            pltpu.VMEM((n_col, 1, cells), F32),
            pltpu.VMEM((n_row, 1, cells), F32),
            pltpu.VMEM((n_col, cells, inner), BF16),
            pltpu.VMEM((n_row, cells, inner), BF16),
            dma,
            dma,
            dma((10,)),
            dma((10,)),
            dma((n_col,)),
            dma((n_col,)),
            dma((n_row,)),
            dma((n_row,)),
            dma((n_col,)),
            dma((n_col,)),
            dma((n_col // 2,)),
            dma((n_col // 2,)),
            dma((n_row,)),
            dma((n_row,)),
        ],
        compiler_params=pltpu.CompilerParams(
            collective_id=0, has_side_effects=True, vmem_limit_bytes=VMEM_LIMIT
        ),
    )(*operands)


def solution(mesh):
    placed = (
        P("row", "col", None),
        P(("row", "col"), None),
        P(),
        P("col"),
        P(),
        P(),
        P(),
        P(),
        P(),
        P(),
        P(),
        P(),
        P("row", "col"),
        P(),
        P(),
    )
    return jax.shard_map(
        functools.partial(per_device, mesh.shape["row"], mesh.shape["col"]),
        mesh=mesh,
        in_specs=placed,
        out_specs=P("row", "col", None),
        check_vma=False,
    )
```

```python
import functools

import jax
import jax.numpy as jnp
from jax import lax
from jax.experimental import pallas as pl
from jax.experimental.pallas import tpu as pltpu
from jax.sharding import PartitionSpec as P

MESH = pl.DeviceIdType.MESH
F32 = jnp.float32
BF16 = jnp.bfloat16
VMEM_LIMIT = 64 * 1024 * 1024


def exact_dot(a, b):
    return jnp.dot(a, b, preferred_element_type=F32, precision=lax.Precision.HIGHEST)


def dot(a, b):
    return jnp.dot(a.astype(BF16), b.astype(BF16), preferred_element_type=F32)


def dot_t(a, b):
    return lax.dot_general(
        a.astype(BF16), b.astype(BF16), (((1,), (1,)), ((), ())), preferred_element_type=F32
    )


def dot_first(a, b):
    return lax.dot_general(
        a.astype(BF16), b.astype(BF16), (((0,), (0,)), ((), ())), preferred_element_type=F32
    )


def split_dot(a, ones):
    high = a.astype(BF16)
    low = (a - high.astype(F32)).astype(BF16)
    both = jnp.dot(jnp.concatenate([high, low], axis=0), ones, preferred_element_type=F32)
    return both[: a.shape[0]] + both[a.shape[0] :]


def silu(v):
    return v / (1.0 + jnp.exp(-v))


def softplus(v):
    return jnp.maximum(v, 0.0) + jnp.log1p(jnp.exp(-jnp.abs(v)))


def kernel(
    n_row,
    n_col,
    *refs,
):
    hbm, out_ref, own = refs[:15], refs[15], refs[16:31]
    (
        latent_ref,
        logs_ref,
        cond_ref,
        trace_ref,
        norm_gain_ref,
        in_ref,
        conv_ref,
        bc_ref,
        dt_ref,
        dt_bias_ref,
        row_rate_ref,
        col_rate_ref,
        horizon_ref,
        out_gain_ref,
        out_weight_ref,
    ) = own
    (
        load_sem,
        shifts,
        lat_f,
        logs_f,
        logs_all,
        logs_flat,
        picks,
        picks_side,
        edge_out,
        edge_line,
        edge_side,
        hz_row,
        hz_col,
        strip_row,
        strip_col,
        logs_send,
        logs_recv,
        edge_send,
        edge_recv,
        hz_send_r,
        hz_recv_r,
        hz_send_c,
        hz_recv_c,
        mix_send_r,
        mix_recv_r,
        pass_send,
        pass_recv,
        mix_send_c,
        mix_recv_c,
    ) = refs[31:]
    rows, cols, width = latent_ref.shape
    cells = rows * cols
    count = n_row * n_col
    inner = in_ref.shape[1] // 2
    heads = dt_bias_ref.shape[1]
    head_dim = inner // heads
    state = bc_ref.shape[1] // 8
    lanes = 4 * heads
    r = lax.axis_index("row")
    c = lax.axis_index("col")
    me = r * n_col + c
    n_token = logs_all.shape[0] * logs_all.shape[1]
    up, down = lax.rem(r + n_row - 1, n_row), lax.rem(r + 1, n_row)
    left, right = lax.rem(c + n_col - 1, n_col), lax.rem(c + 1, n_col)

    barrier = pltpu.get_barrier_semaphore()

    loads = [
        pltpu.make_async_copy(hbm[k], own[k], load_sem.at[k]) for k in range(len(hbm))
    ]
    for k in (0, 1, 12, 3, 2, 5, 4, 6, 7, 8, 9, 10, 11, 13, 14):
        loads[k].start()

    row_of = [lax.rem(r + o, n_row) for o in range(n_row)]
    col_of = [lax.rem(c + o, n_col) for o in range(n_col)]
    others = [(i, j) for i in range(n_row) for j in range(n_col) if i + j > 0]
    for i, j in others:
        pl.semaphore_signal(
            barrier, inc=1, device_id=(row_of[i], col_of[j]), device_id_type=MESH
        )

    for k in (0, 1, 3, 12):
        loads[k].wait()
    lat = latent_ref[...].astype(F32)
    lat_f[...] = lat
    edge_out[0] = lat_f[:, 0, :]
    edge_out[1] = lat_f[:, cols - 1, :]
    logs_f[...] = logs_ref[...].astype(F32)
    logs_all[me] = logs_f[...]
    sub = lax.broadcasted_iota(jnp.int32, (cols, n_token), 0)
    lane = lax.broadcasted_iota(jnp.int32, (cols, n_token), 1)
    want = jnp.zeros((cols, n_token), jnp.int32)
    for j in range(cols):
        want = jnp.where(sub == j, trace_ref[j], want)
    picks[...] = (want == lane).astype(F32)
    line_pick = (
        lax.broadcasted_iota(jnp.int32, (rows, cells), 1) // cols
        == lax.broadcasted_iota(jnp.int32, (rows, cells), 0)
    ).astype(F32)
    column_pick = lax.rem(
        lax.broadcasted_iota(jnp.int32, (cols, cells), 1), cols
    ) == lax.broadcasted_iota(jnp.int32, (cols, cells), 0)
    marks = jnp.sum(
        jnp.where(column_pick, exact_dot(horizon_ref[...], line_pick), 0.0), axis=0, keepdims=True
    )
    hz_row[c] = marks
    hz_col[r] = marks

    pl.semaphore_wait(barrier, count - 1)

    for i, j in others:
        pltpu.make_async_remote_copy(
            src_ref=logs_f,
            dst_ref=logs_all.at[me],
            send_sem=logs_send,
            recv_sem=logs_recv,
            device_id=(row_of[i], col_of[j]),
            device_id_type=MESH,
        ).start()

    last = rows - 1
    edges = []
    for src, dst, to in (
        (picks, picks_side.at[0], (r, right)),
        (picks, picks_side.at[1], (r, left)),
        (edge_out.at[1], edge_side.at[0], (r, right)),
        (edge_out.at[0], edge_side.at[1], (r, left)),
        (lat_f.at[last], edge_line.at[0], (down, c)),
        (lat_f.at[last], edge_line.at[1], (down, right)),
        (lat_f.at[last], edge_line.at[2], (down, left)),
        (lat_f.at[0], edge_line.at[3], (up, c)),
        (lat_f.at[0], edge_line.at[4], (up, right)),
        (lat_f.at[0], edge_line.at[5], (up, left)),
    ):
        k = len(edges)
        edges.append(
            pltpu.make_async_remote_copy(
                src_ref=src,
                dst_ref=dst,
                send_sem=edge_send.at[k],
                recv_sem=edge_recv.at[k],
                device_id=to,
                device_id_type=MESH,
            )
        )
        edges[-1].start()

    def fan(buffer, place, n, axis, send, recv, step):
        copies = []
        for o in range(step, n, step):
            to = lax.rem(place + o, n)
            copies.append(
                pltpu.make_async_remote_copy(
                    src_ref=buffer.at[place],
                    dst_ref=buffer.at[place],
                    send_sem=send.at[o],
                    recv_sem=recv.at[o],
                    device_id=(to, c) if axis == 0 else (r, to),
                    device_id_type=MESH,
                )
            )
            copies[-1].start()
        return copies

    hz_copies = fan(hz_row, c, n_col, 1, hz_send_r, hz_recv_r, 1)
    hz_copies += fan(hz_col, r, n_row, 0, hz_send_c, hz_recv_c, 1)

    lane_head = lax.rem(lax.broadcasted_iota(jnp.int32, (lanes, heads), 0), heads)
    spread = (lane_head == lax.broadcasted_iota(jnp.int32, (lanes, heads), 1)).astype(F32)

    def lane_column(table, first):
        wide = lax.dot_general(
            spread,
            table,
            (((1,), (1,)), ((), ())),
            preferred_element_type=F32,
            precision=lax.Precision.HIGHEST,
        )
        kind = lax.broadcasted_iota(jnp.int32, wide.shape, 0) // heads
        own = lax.broadcasted_iota(jnp.int32, wide.shape, 1) + first
        return jnp.sum(jnp.where(kind == own, wide, 0.0), axis=1, keepdims=True)

    for k in (9, 10, 11):
        loads[k].wait()
    bias = lane_column(dt_bias_ref[...], 0)
    rates = lane_column(row_rate_ref[...] / (16.0 * cols * n_col), 0) + lane_column(
        col_rate_ref[...] / (16.0 * rows * n_row), 2
    )
    expand = (
        lax.broadcasted_iota(jnp.int32, (heads, inner), 0)
        == lax.broadcasted_iota(jnp.int32, (heads, inner), 1) // head_dim
    ).astype(BF16)

    cell_0 = lax.broadcasted_iota(jnp.int32, (cells, cells), 0)
    cell_1 = lax.broadcasted_iota(jnp.int32, (cells, cells), 1)
    i0, j0 = cell_0 // cols, lax.rem(cell_0, cols)
    i1, j1 = cell_1 // cols, lax.rem(cell_1, cols)

    n_src = cells + 6 * cols + 2 * rows
    src_id = lax.broadcasted_iota(jnp.int32, (cells, n_src), 1)
    cell_id = lax.broadcasted_iota(jnp.int32, (cells, 1), 0)
    ci, cj = cell_id // cols, lax.rem(cell_id, cols)
    for a in range(3):
        for b in range(3):
            pi, pj = ci + a - 1, cj + b - 1
            row_in = (pi >= 0) & (pi < rows)
            where_from = pi * cols + pj
            line_base = jnp.where(pi < 0, cells, cells + 3 * cols)
            line_from = line_base + jnp.where(
                pj < 0, 2 * cols - 1, jnp.where(pj >= cols, 2 * cols, pj)
            )
            side_from = cells + 6 * cols + pi + jnp.where(pj < 0, 0, rows)
            source = jnp.where(
                row_in, jnp.where((pj >= 0) & (pj < cols), where_from, side_from), line_from
            )
            gi, gj = r * rows + pi, c * cols + pj
            inside = (gi >= 0) & (gi < n_row * rows) & (gj >= 0) & (gj < n_col * cols)
            source = jnp.where(inside, source, -1)
            shifts[3 * a + b] = (src_id == source).astype(BF16)

    def wait_for(part, sem):
        pltpu.make_async_copy(part, part, sem).wait()

    arrived = logs_all.at[pl.ds(0, count - 1)]
    wait_for(arrived, logs_recv)
    wait_for(arrived, logs_send)
    per = logs_all.shape[1]
    for k in range(logs_all.shape[0]):
        logs_flat[pl.ds(k * per, per), :] = logs_all[k]
    loads[2].wait()
    tokens = silu(dot(logs_flat[...], cond_ref[...])).astype(BF16)

    for edge in edges:
        edge.wait()
    own_tokens = dot(picks[...], tokens)
    left_tokens = dot(picks_side[0], tokens)
    right_tokens = dot(picks_side[1], tokens)

    hidden_own = (lat_f[...] + own_tokens[None]).reshape(cells, width)
    left_token = left_tokens[cols - 1 : cols]
    right_token = right_tokens[0:1]
    hidden = jnp.concatenate(
        [
            hidden_own,
            edge_line[0] + own_tokens,
            edge_line[1] + left_tokens,
            edge_line[2] + right_tokens,
            edge_line[3] + own_tokens,
            edge_line[4] + left_tokens,
            edge_line[5] + right_tokens,
            edge_side[0] + left_token,
            edge_side[1] + right_token,
        ],
        axis=0,
    )
    for k in (4, 5, 6):
        loads[k].wait()
    normed = (
        hidden
        * lax.rsqrt(jnp.mean(hidden * hidden, axis=-1, keepdims=True) + 1e-06)
        * norm_gain_ref[...]
    ).astype(BF16)
    pre_conv = dot(normed, in_ref[:, :inner]).astype(BF16)
    gate_part = dot(normed[:cells], in_ref[:, inner:]).astype(BF16)
    conv_sum = jnp.zeros((cells, inner), F32)
    for k in range(9):
        conv_sum = conv_sum + dot(shifts[k], pre_conv) * conv_ref[k : k + 1, :]
    mixed = silu(conv_sum).astype(BF16)
    strip_row[c] = mixed
    strip_col[r] = mixed
    sibling = c + 1 - 2 * lax.rem(c, 2)

    def to_sibling(e):
        place = lax.rem(c + n_col - 2 * e, n_col)
        return pltpu.make_async_remote_copy(
            src_ref=strip_row.at[place],
            dst_ref=strip_row.at[place],
            send_sem=pass_send.at[e],
            recv_sem=pass_recv.at[e],
            device_id=(r, sibling),
            device_id_type=MESH,
        )

    row_copies = fan(strip_row, c, n_col, 1, mix_send_r, mix_recv_r, 2)
    col_copies = fan(strip_col, r, n_row, 0, mix_send_c, mix_recv_c, 1)
    passed = [to_sibling(e) for e in range(n_col // 2)]
    passed[0].start()

    mixed_f = mixed.astype(F32)
    loads[7].wait()
    loads[8].wait()
    coefs = dot(mixed, bc_ref[...]).astype(BF16)
    in_coef = [coefs[:, 2 * k * state : (2 * k + 1) * state] for k in range(4)]
    out_coef = [coefs[:, (2 * k + 1) * state : (2 * k + 2) * state] for k in range(4)]

    def steps_of(x, marks, first, last):
        step = softplus(dot_t(dt_ref[first:last, :], x) + bias[first:last])
        return step, -step * rates[first:last] - marks

    step, decay = steps_of(mixed, marks, 0, lanes)
    total = jnp.zeros((cells, inner), F32)
    entry = []
    for k in range(4):
        if k < 2:
            same, p0, p1, length = i0 == i1, j0, j1, cols
        else:
            same, p0, p1, length = j0 == j1, i0, i1, rows
        if k % 2 == 1:
            p0, p1 = length - 1 - p0, length - 1 - p1
        halves = []
        while length > 1:
            length //= 2
            halves.append(length)
        reach = []
        for half in halves:
            block = (p0 // half) == (p1 // half)
            late = lax.rem(p1 // half, 2) == 1
            reach.append(same & block & ((late & (p0 <= p1)) | (~late & (p0 > p1))))
        reach.append(same & (p0 <= p1))
        sums = split_dot(
            decay[k * heads : (k + 1) * heads],
            jnp.concatenate([one.astype(BF16) for one in reach], axis=1),
        )
        own_step = step[k * heads : (k + 1) * heads]
        factor = jnp.exp(sums[:, : len(halves) * cells])
        wide = dot_first(
            jnp.concatenate(
                [factor, factor * jnp.tile(own_step, (1, len(halves))), own_step], axis=1
            ),
            expand,
        )
        wide = [wide[n * cells : (n + 1) * cells] for n in range(2 * len(halves) + 1)]
        scores = dot_t(out_coef[k], in_coef[k])
        total = total + dot(jnp.where(cell_0 == cell_1, scores, 0.0), mixed_f * wide[-1])
        for n, half in enumerate(halves):
            b0, b1 = p0 // half, p1 // half
            pair = same & (b0 == b1 + 1) & (lax.rem(b0, 2) == 1)
            total = total + wide[n] * dot(
                jnp.where(pair, scores, 0.0), mixed_f * wide[len(halves) + n]
            )
        entry.append(sums[:, len(halves) * cells :])

    def entering(first, strip, marks, place, tiles, same, later):
        after = (same & (later > 0)).astype(BF16)
        before = (same & (later < 0)).astype(BF16)
        whole = same.astype(BF16)
        n = len(tiles)
        xs = [strip[q] for q in tiles]
        marks = jnp.concatenate([marks[q] for q in tiles], axis=1)
        step, decay = steps_of(
            jnp.concatenate(xs, axis=0), marks, first * heads, (first + 2) * heads
        )
        tile = [slice(m * cells, (m + 1) * cells) for m in range(n)]

        def stacked(part, ones):
            sums = split_dot(
                jnp.concatenate([part[:, tile[m]] for m in range(n)], axis=0),
                jnp.concatenate([ones, whole], axis=1),
            )
            sums = [sums[m * heads : (m + 1) * heads] for m in range(n)]
            return [one[:, :cells] for one in sums], [one[:, cells:] for one in sums]

        sums_f, totals_f = stacked(decay[:heads], after)
        sums_b, totals_b = stacked(decay[heads:], before)
        gains = []
        for m, q in enumerate(tiles):
            gain = jnp.where(q < place, step[:heads, tile[m]], step[heads:, tile[m]])
            gains.append(gain * jnp.exp(jnp.where(q < place, sums_f[m], sums_b[m])))
        wide = dot_first(jnp.concatenate(gains, axis=1), expand)
        weight_f = bc_ref[:, 2 * first * state : (2 * first + 1) * state]
        weight_b = bc_ref[:, (2 * first + 2) * state : (2 * first + 3) * state]
        out = []
        for m, q in enumerate(tiles):
            ahead = q < place
            driven = xs[m].astype(F32) * wide[tile[m]]
            coef = dot(xs[m], jnp.where(ahead, weight_f, weight_b))
            reader = jnp.where(ahead, out_coef[first], out_coef[first + 1])
            scores = jnp.where(same, dot_t(reader, coef), 0.0)
            out.append((q, jnp.where(ahead, totals_f[m], totals_b[m]), dot(scores, driven)))
        return out

    def decayed(first, place, parts):
        exponents = []
        for q, _, _ in parts:
            exponent = jnp.where(q < place, entry[first], entry[first + 1])
            for other, between, _ in parts:
                inner_f = (q < other) & (other < place)
                inner_b = (q > other) & (other > place)
                exponent = exponent + jnp.where(inner_f | inner_b, between, 0.0)
            exponents.append(exponent)
        wide = dot_first(jnp.exp(jnp.concatenate(exponents, axis=1)), expand)
        inflow = jnp.zeros((cells, inner), F32)
        for m, (_, _, part) in enumerate(parts):
            inflow = inflow + wide[m * cells : (m + 1) * cells] * part
        return inflow

    for copy in hz_copies:
        copy.wait()
    for copy in col_copies:
        copy.wait()
    others_r = [lax.rem(r + n_row - o, n_row) for o in range(1, n_row)]
    total = total + decayed(
        2, r, entering(2, strip_col, hz_col, r, others_r, j0 == j1, i0 - i1)
    )
    passed[0].wait()
    parts = entering(0, strip_row, hz_row, c, [sibling], i0 == i1, j0 - j1)
    for e, copy in enumerate(row_copies):
        copy.wait()
        passed[e + 1].start()
    near = [lax.rem(c + n_col - o, n_col) for o in range(2, n_col, 2)]
    far = [lax.rem(sibling + n_col - o, n_col) for o in range(2, n_col, 2)]
    parts += entering(0, strip_row, hz_row, c, near, i0 == i1, j0 - j1)
    for copy in passed[1:]:
        copy.wait()
    parts += entering(0, strip_row, hz_row, c, far, i0 == i1, j0 - j1)
    total = total + decayed(0, c, parts)

    loads[13].wait()
    loads[14].wait()
    gated = (
        total
        * lax.rsqrt(jnp.mean(total * total, axis=-1, keepdims=True) + 1e-05)
        * out_gain_ref[...]
        * silu(gate_part.astype(F32))
    ).astype(BF16)
    result = hidden_own + dot(gated, out_weight_ref[...])
    out_ref[...] = result.reshape(rows, cols, width)


def per_device(n_row, n_col, *args):
    (
        latent,
        logs,
        cond,
        trace,
        norm_gain,
        in_weight,
        conv,
        bc,
        dt,
        dt_bias,
        row_rate,
        col_rate,
        horizon,
        out_gain,
        out_weight,
    ) = args
    rows, cols, width = latent.shape
    inner = in_weight.shape[1] // 2
    cells = rows * cols
    count = n_row * n_col
    per = logs.shape[0]
    vmem = pl.BlockSpec(memory_space=pltpu.VMEM)
    operands = (
        latent,
        logs,
        cond,
        trace,
        norm_gain.reshape(1, width),
        in_weight,
        conv,
        bc,
        dt.T,
        dt_bias,
        row_rate,
        col_rate,
        horizon.T,
        out_gain.reshape(1, inner),
        out_weight,
    )
    own = [pltpu.VMEM(one.shape, one.dtype) for one in operands]
    own[3] = pltpu.SMEM(trace.shape, trace.dtype)
    dma = pltpu.SemaphoreType.DMA
    return pl.pallas_call(
        functools.partial(kernel, n_row, n_col),
        out_shape=jax.ShapeDtypeStruct((rows, cols, width), F32),
        in_specs=[pl.BlockSpec(memory_space=pltpu.HBM)] * len(operands),
        out_specs=vmem,
        scratch_shapes=own
        + [
            dma((len(operands),)),
            pltpu.VMEM((9, cells, cells + 6 * cols + 2 * rows), BF16),
            pltpu.VMEM((rows, cols, width), F32),
            pltpu.VMEM((per, width), F32),
            pltpu.VMEM((count, per, width), F32),
            pltpu.VMEM((count * per, width), F32),
            pltpu.VMEM((cols, count * per), F32),
            pltpu.VMEM((2, cols, count * per), F32),
            pltpu.VMEM((2, rows, width), F32),
            pltpu.VMEM((6, cols, width), F32),
            pltpu.VMEM((2, rows, width), F32),
            pltpu.VMEM((n_col, 1, cells), F32),
            pltpu.VMEM((n_row, 1, cells), F32),
            pltpu.VMEM((n_col, cells, inner), BF16),
            pltpu.VMEM((n_row, cells, inner), BF16),
            dma,
            dma,
            dma((10,)),
            dma((10,)),
            dma((n_col,)),
            dma((n_col,)),
            dma((n_row,)),
            dma((n_row,)),
            dma((n_col,)),
            dma((n_col,)),
            dma((n_col // 2,)),
            dma((n_col // 2,)),
            dma((n_row,)),
            dma((n_row,)),
        ],
        compiler_params=pltpu.CompilerParams(
            collective_id=0, has_side_effects=True, vmem_limit_bytes=VMEM_LIMIT
        ),
    )(*operands).astype(BF16)


def solution(mesh):
    placed = (
        P("row", "col", None),
        P(("row", "col"), None),
        P(),
        P("col"),
        P(),
        P(),
        P(),
        P(),
        P(),
        P(),
        P(),
        P(),
        P("row", "col"),
        P(),
        P(),
    )
    return jax.shard_map(
        functools.partial(per_device, mesh.shape["row"], mesh.shape["col"]),
        mesh=mesh,
        in_specs=placed,
        out_specs=P("row", "col", None),
        check_vma=False,
    )
```

```python
import functools

import jax
import jax.numpy as jnp
from jax import lax
from jax.experimental import pallas as pl
from jax.experimental.pallas import tpu as pltpu
from jax.sharding import PartitionSpec as P

MESH = pl.DeviceIdType.MESH
F32 = jnp.float32
BF16 = jnp.bfloat16
VMEM_LIMIT = 64 * 1024 * 1024


def exact_dot(a, b):
    return jnp.dot(a, b, preferred_element_type=F32, precision=lax.Precision.HIGHEST)


def dot(a, b):
    return jnp.dot(a.astype(BF16), b.astype(BF16), preferred_element_type=F32)


def dot_t(a, b):
    return lax.dot_general(
        a.astype(BF16), b.astype(BF16), (((1,), (1,)), ((), ())), preferred_element_type=F32
    )


def dot_first(a, b):
    return lax.dot_general(
        a.astype(BF16), b.astype(BF16), (((0,), (0,)), ((), ())), preferred_element_type=F32
    )


def split_dot(a, ones):
    high = a.astype(BF16)
    low = (a - high.astype(F32)).astype(BF16)
    both = jnp.dot(jnp.concatenate([high, low], axis=0), ones, preferred_element_type=F32)
    return both[: a.shape[0]] + both[a.shape[0] :]


def silu(v):
    return v / (1.0 + jnp.exp(-v))


def softplus(v):
    return jnp.maximum(v, 0.0) + jnp.log1p(jnp.exp(-jnp.abs(v)))


def levels(length):
    return length.bit_length() - 1


def kernel(
    n_row,
    n_col,
    *refs,
):
    hbm, out_ref, own = refs[:15], refs[15], refs[16:31]
    (
        latent_ref,
        logs_ref,
        cond_ref,
        trace_ref,
        norm_gain_ref,
        in_ref,
        conv_ref,
        bc_ref,
        dt_ref,
        dt_bias_ref,
        row_rate_ref,
        col_rate_ref,
        horizon_ref,
        out_gain_ref,
        out_weight_ref,
    ) = own
    (
        load_sem,
        shifts,
        reach_all,
        pair_all,
        order_all,
        lat_f,
        logs_f,
        logs_all,
        logs_flat,
        picks,
        picks_side,
        edge_out,
        edge_line,
        edge_side,
        hz_row,
        hz_col,
        strip_row,
        strip_col,
        logs_send,
        logs_recv,
        edge_send,
        edge_recv,
        hz_send_r,
        hz_recv_r,
        hz_send_c,
        hz_recv_c,
        mix_send_r,
        mix_recv_r,
        pass_send,
        pass_recv,
        mix_send_c,
        mix_recv_c,
    ) = refs[31:]
    rows, cols, width = latent_ref.shape
    cells = rows * cols
    count = n_row * n_col
    inner = in_ref.shape[1] // 2
    heads = dt_bias_ref.shape[1]
    head_dim = inner // heads
    state = bc_ref.shape[1] // 8
    lanes = 4 * heads
    r = lax.axis_index("row")
    c = lax.axis_index("col")
    me = r * n_col + c
    n_token = logs_all.shape[0] * logs_all.shape[1]
    up, down = lax.rem(r + n_row - 1, n_row), lax.rem(r + 1, n_row)
    left, right = lax.rem(c + n_col - 1, n_col), lax.rem(c + 1, n_col)

    barrier = pltpu.get_barrier_semaphore()

    loads = [
        pltpu.make_async_copy(hbm[k], own[k], load_sem.at[k]) for k in range(len(hbm))
    ]
    for k in (0, 1, 12, 3, 2, 5, 4, 6, 7, 8, 9, 10, 11, 13, 14):
        loads[k].start()

    row_of = [lax.rem(r + o, n_row) for o in range(n_row)]
    col_of = [lax.rem(c + o, n_col) for o in range(n_col)]
    others = [(i, j) for i in range(n_row) for j in range(n_col) if i + j > 0]
    for i, j in others:
        pl.semaphore_signal(
            barrier, inc=1, device_id=(row_of[i], col_of[j]), device_id_type=MESH
        )

    for k in (0, 1, 3, 12):
        loads[k].wait()
    lat = latent_ref[...].astype(F32)
    lat_f[...] = lat
    edge_out[0] = lat_f[:, 0, :]
    edge_out[1] = lat_f[:, cols - 1, :]
    logs_f[...] = logs_ref[...].astype(F32)
    logs_all[me] = logs_f[...]
    sub = lax.broadcasted_iota(jnp.int32, (cols, n_token), 0)
    lane = lax.broadcasted_iota(jnp.int32, (cols, n_token), 1)
    want = jnp.zeros((cols, n_token), jnp.int32)
    for j in range(cols):
        want = jnp.where(sub == j, trace_ref[j], want)
    picks[...] = (want == lane).astype(F32)
    line_pick = (
        lax.broadcasted_iota(jnp.int32, (rows, cells), 1) // cols
        == lax.broadcasted_iota(jnp.int32, (rows, cells), 0)
    ).astype(F32)
    column_pick = lax.rem(
        lax.broadcasted_iota(jnp.int32, (cols, cells), 1), cols
    ) == lax.broadcasted_iota(jnp.int32, (cols, cells), 0)
    marks = jnp.sum(
        jnp.where(column_pick, exact_dot(horizon_ref[...], line_pick), 0.0), axis=0, keepdims=True
    )
    hz_row[c] = marks
    hz_col[r] = marks

    pl.semaphore_wait(barrier, count - 1)

    for i, j in others:
        pltpu.make_async_remote_copy(
            src_ref=logs_f,
            dst_ref=logs_all.at[me],
            send_sem=logs_send,
            recv_sem=logs_recv,
            device_id=(row_of[i], col_of[j]),
            device_id_type=MESH,
        ).start()

    last = rows - 1
    edges = []
    for src, dst, to in (
        (picks, picks_side.at[0], (r, right)),
        (picks, picks_side.at[1], (r, left)),
        (edge_out.at[1], edge_side.at[0], (r, right)),
        (edge_out.at[0], edge_side.at[1], (r, left)),
        (lat_f.at[last], edge_line.at[0], (down, c)),
        (lat_f.at[last], edge_line.at[1], (down, right)),
        (lat_f.at[last], edge_line.at[2], (down, left)),
        (lat_f.at[0], edge_line.at[3], (up, c)),
        (lat_f.at[0], edge_line.at[4], (up, right)),
        (lat_f.at[0], edge_line.at[5], (up, left)),
    ):
        k = len(edges)
        edges.append(
            pltpu.make_async_remote_copy(
                src_ref=src,
                dst_ref=dst,
                send_sem=edge_send.at[k],
                recv_sem=edge_recv.at[k],
                device_id=to,
                device_id_type=MESH,
            )
        )
        edges[-1].start()

    def fan(buffer, place, n, axis, send, recv, step):
        copies = []
        for o in range(step, n, step):
            to = lax.rem(place + o, n)
            copies.append(
                pltpu.make_async_remote_copy(
                    src_ref=buffer.at[place],
                    dst_ref=buffer.at[place],
                    send_sem=send.at[o],
                    recv_sem=recv.at[o],
                    device_id=(to, c) if axis == 0 else (r, to),
                    device_id_type=MESH,
                )
            )
            copies[-1].start()
        return copies

    hz_copies = fan(hz_row, c, n_col, 1, hz_send_r, hz_recv_r, 1)
    hz_copies += fan(hz_col, r, n_row, 0, hz_send_c, hz_recv_c, 1)

    lane_head = lax.rem(lax.broadcasted_iota(jnp.int32, (lanes, heads), 0), heads)
    spread = (lane_head == lax.broadcasted_iota(jnp.int32, (lanes, heads), 1)).astype(F32)

    def lane_column(table, first):
        wide = lax.dot_general(
            spread,
            table,
            (((1,), (1,)), ((), ())),
            preferred_element_type=F32,
            precision=lax.Precision.HIGHEST,
        )
        kind = lax.broadcasted_iota(jnp.int32, wide.shape, 0) // heads
        own = lax.broadcasted_iota(jnp.int32, wide.shape, 1) + first
        return jnp.sum(jnp.where(kind == own, wide, 0.0), axis=1, keepdims=True)

    for k in (9, 10, 11):
        loads[k].wait()
    bias = lane_column(dt_bias_ref[...], 0)
    rates = lane_column(row_rate_ref[...] / (16.0 * cols * n_col), 0) + lane_column(
        col_rate_ref[...] / (16.0 * rows * n_row), 2
    )
    expand = (
        lax.broadcasted_iota(jnp.int32, (heads, inner), 0)
        == lax.broadcasted_iota(jnp.int32, (heads, inner), 1) // head_dim
    ).astype(BF16)

    cell_0 = lax.broadcasted_iota(jnp.int32, (cells, cells), 0)
    cell_1 = lax.broadcasted_iota(jnp.int32, (cells, cells), 1)
    i0, j0 = cell_0 // cols, lax.rem(cell_0, cols)
    i1, j1 = cell_1 // cols, lax.rem(cell_1, cols)

    pair_all[0] = (cell_0 == cell_1).astype(BF16)
    halves_of, first_pair, pairs = [], [], 1
    for k in range(4):
        if k < 2:
            same, p0, p1, length = i0 == i1, j0, j1, cols
        else:
            same, p0, p1, length = j0 == j1, i0, i1, rows
        if k % 2 == 1:
            p0, p1 = length - 1 - p0, length - 1 - p1
        halves = []
        while length > 1:
            length //= 2
            halves.append(length)
        halves_of.append(halves)
        first_pair.append(pairs)
        for n, half in enumerate(halves):
            b0, b1 = p0 // half, p1 // half
            late = lax.rem(b1, 2) == 1
            reach = same & (b0 == b1) & ((late & (p0 <= p1)) | (~late & (p0 > p1)))
            reach_all[k, :, n * cells : (n + 1) * cells] = reach.astype(BF16)
            pair = same & (b0 == b1 + 1) & (lax.rem(b0, 2) == 1)
            pair_all[pairs] = pair.astype(BF16)
            pairs += 1
        reach = (same & (p0 <= p1)).astype(BF16)
        reach_all[k, :, len(halves) * cells : (len(halves) + 1) * cells] = reach
    for k, (same, later) in enumerate(((i0 == i1, j0 - j1), (j0 == j1, i0 - i1))):
        order_all[k, 0] = (same & (later > 0)).astype(BF16)
        order_all[k, 1] = (same & (later < 0)).astype(BF16)
        order_all[k, 2] = same.astype(BF16)

    n_src = cells + 6 * cols + 2 * rows
    src_id = lax.broadcasted_iota(jnp.int32, (cells, n_src), 1)
    cell_id = lax.broadcasted_iota(jnp.int32, (cells, 1), 0)
    ci, cj = cell_id // cols, lax.rem(cell_id, cols)
    for a in range(3):
        for b in range(3):
            pi, pj = ci + a - 1, cj + b - 1
            row_in = (pi >= 0) & (pi < rows)
            where_from = pi * cols + pj
            line_base = jnp.where(pi < 0, cells, cells + 3 * cols)
            line_from = line_base + jnp.where(
                pj < 0, 2 * cols - 1, jnp.where(pj >= cols, 2 * cols, pj)
            )
            side_from = cells + 6 * cols + pi + jnp.where(pj < 0, 0, rows)
            source = jnp.where(
                row_in, jnp.where((pj >= 0) & (pj < cols), where_from, side_from), line_from
            )
            gi, gj = r * rows + pi, c * cols + pj
            inside = (gi >= 0) & (gi < n_row * rows) & (gj >= 0) & (gj < n_col * cols)
            source = jnp.where(inside, source, -1)
            shifts[3 * a + b] = (src_id == source).astype(BF16)

    def wait_for(part, sem):
        pltpu.make_async_copy(part, part, sem).wait()

    arrived = logs_all.at[pl.ds(0, count - 1)]
    wait_for(arrived, logs_recv)
    wait_for(arrived, logs_send)
    per = logs_all.shape[1]
    for k in range(logs_all.shape[0]):
        logs_flat[pl.ds(k * per, per), :] = logs_all[k]
    loads[2].wait()
    tokens = silu(dot(logs_flat[...], cond_ref[...])).astype(BF16)

    for edge in edges:
        edge.wait()
    own_tokens = dot(picks[...], tokens)
    left_tokens = dot(picks_side[0], tokens)
    right_tokens = dot(picks_side[1], tokens)

    hidden_own = (lat_f[...] + own_tokens[None]).reshape(cells, width)
    left_token = left_tokens[cols - 1 : cols]
    right_token = right_tokens[0:1]
    hidden = jnp.concatenate(
        [
            hidden_own,
            edge_line[0] + own_tokens,
            edge_line[1] + left_tokens,
            edge_line[2] + right_tokens,
            edge_line[3] + own_tokens,
            edge_line[4] + left_tokens,
            edge_line[5] + right_tokens,
            edge_side[0] + left_token,
            edge_side[1] + right_token,
        ],
        axis=0,
    )
    for k in (4, 5, 6):
        loads[k].wait()
    normed = (
        hidden
        * lax.rsqrt(jnp.mean(hidden * hidden, axis=-1, keepdims=True) + 1e-06)
        * norm_gain_ref[...]
    ).astype(BF16)
    pre_conv = dot(normed, in_ref[:, :inner]).astype(BF16)
    gate_part = dot(normed[:cells], in_ref[:, inner:]).astype(BF16)
    conv_sum = jnp.zeros((cells, inner), F32)
    for k in range(9):
        conv_sum = conv_sum + dot(shifts[k], pre_conv) * conv_ref[k : k + 1, :]
    mixed = silu(conv_sum).astype(BF16)
    strip_row[c] = mixed
    strip_col[r] = mixed
    sibling = c + 1 - 2 * lax.rem(c, 2)

    def to_sibling(e):
        place = lax.rem(c + n_col - 2 * e, n_col)
        return pltpu.make_async_remote_copy(
            src_ref=strip_row.at[place],
            dst_ref=strip_row.at[place],
            send_sem=pass_send.at[e],
            recv_sem=pass_recv.at[e],
            device_id=(r, sibling),
            device_id_type=MESH,
        )

    row_copies = fan(strip_row, c, n_col, 1, mix_send_r, mix_recv_r, 2)
    col_copies = fan(strip_col, r, n_row, 0, mix_send_c, mix_recv_c, 1)
    passed = [to_sibling(e) for e in range(n_col // 2)]
    passed[0].start()

    mixed_f = mixed.astype(F32)
    loads[7].wait()
    loads[8].wait()
    coefs = dot(mixed, bc_ref[...]).astype(BF16)
    in_coef = [coefs[:, 2 * k * state : (2 * k + 1) * state] for k in range(4)]
    out_coef = [coefs[:, (2 * k + 1) * state : (2 * k + 2) * state] for k in range(4)]

    def steps_of(x, marks, first, last):
        step = softplus(dot_t(dt_ref[first:last, :], x) + bias[first:last])
        return step, -step * rates[first:last] - marks

    step, decay = steps_of(mixed, marks, 0, lanes)
    total = jnp.zeros((cells, inner), F32)
    entry = []
    for k in range(4):
        halves = halves_of[k]
        sums = split_dot(
            decay[k * heads : (k + 1) * heads],
            reach_all[k, :, : (len(halves) + 1) * cells],
        )
        own_step = step[k * heads : (k + 1) * heads]
        factor = jnp.exp(sums[:, : len(halves) * cells])
        wide = dot_first(
            jnp.concatenate(
                [factor, factor * jnp.tile(own_step, (1, len(halves))), own_step], axis=1
            ),
            expand,
        )
        wide = [wide[n * cells : (n + 1) * cells] for n in range(2 * len(halves) + 1)]
        scores = dot_t(out_coef[k], in_coef[k]).astype(BF16)
        total = total + dot(scores * pair_all[0], mixed_f * wide[-1])
        for n in range(len(halves)):
            total = total + wide[n] * dot(
                scores * pair_all[first_pair[k] + n], mixed_f * wide[len(halves) + n]
            )
        entry.append(sums[:, len(halves) * cells :])

    def entering(first, strip, marks, place, tiles):
        after, before, whole = (order_all[first // 2, k] for k in range(3))
        n = len(tiles)
        xs = [strip[q] for q in tiles]
        marks = jnp.concatenate([marks[q] for q in tiles], axis=1)
        step, decay = steps_of(
            jnp.concatenate(xs, axis=0), marks, first * heads, (first + 2) * heads
        )
        tile = [slice(m * cells, (m + 1) * cells) for m in range(n)]

        def stacked(part, ones):
            sums = split_dot(
                jnp.concatenate([part[:, tile[m]] for m in range(n)], axis=0),
                jnp.concatenate([ones, whole], axis=1),
            )
            sums = [sums[m * heads : (m + 1) * heads] for m in range(n)]
            return [one[:, :cells] for one in sums], [one[:, cells:] for one in sums]

        sums_f, totals_f = stacked(decay[:heads], after)
        sums_b, totals_b = stacked(decay[heads:], before)
        gains = []
        for m, q in enumerate(tiles):
            gain = jnp.where(q < place, step[:heads, tile[m]], step[heads:, tile[m]])
            gains.append(gain * jnp.exp(jnp.where(q < place, sums_f[m], sums_b[m])))
        wide = dot_first(jnp.concatenate(gains, axis=1), expand)
        weight_f = bc_ref[:, 2 * first * state : (2 * first + 1) * state]
        weight_b = bc_ref[:, (2 * first + 2) * state : (2 * first + 3) * state]
        out = []
        for m, q in enumerate(tiles):
            ahead = q < place
            driven = xs[m].astype(F32) * wide[tile[m]]
            coef = dot(xs[m], jnp.where(ahead, weight_f, weight_b))
            reader = jnp.where(ahead, out_coef[first], out_coef[first + 1])
            scores = dot_t(reader, coef).astype(BF16) * whole
            out.append((q, jnp.where(ahead, totals_f[m], totals_b[m]), dot(scores, driven)))
        return out

    def decayed(first, place, parts):
        exponents = []
        for q, _, _ in parts:
            exponent = jnp.where(q < place, entry[first], entry[first + 1])
            for other, between, _ in parts:
                inner_f = (q < other) & (other < place)
                inner_b = (q > other) & (other > place)
                exponent = exponent + jnp.where(inner_f | inner_b, between, 0.0)
            exponents.append(exponent)
        wide = dot_first(jnp.exp(jnp.concatenate(exponents, axis=1)), expand)
        inflow = jnp.zeros((cells, inner), F32)
        for m, (_, _, part) in enumerate(parts):
            inflow = inflow + wide[m * cells : (m + 1) * cells] * part
        return inflow

    for copy in hz_copies:
        copy.wait()
    for copy in col_copies:
        copy.wait()
    others_r = [lax.rem(r + n_row - o, n_row) for o in range(1, n_row)]
    total = total + decayed(
        2, r, entering(2, strip_col, hz_col, r, others_r)
    )
    passed[0].wait()
    parts = entering(0, strip_row, hz_row, c, [sibling])
    for e, copy in enumerate(row_copies):
        copy.wait()
        passed[e + 1].start()
    near = [lax.rem(c + n_col - o, n_col) for o in range(2, n_col, 2)]
    far = [lax.rem(sibling + n_col - o, n_col) for o in range(2, n_col, 2)]
    parts += entering(0, strip_row, hz_row, c, near)
    for copy in passed[1:]:
        copy.wait()
    parts += entering(0, strip_row, hz_row, c, far)
    total = total + decayed(0, c, parts)

    loads[13].wait()
    loads[14].wait()
    gated = (
        total
        * lax.rsqrt(jnp.mean(total * total, axis=-1, keepdims=True) + 1e-05)
        * out_gain_ref[...]
        * silu(gate_part.astype(F32))
    ).astype(BF16)
    result = hidden_own + dot(gated, out_weight_ref[...])
    out_ref[...] = result.reshape(rows, cols, width)


def per_device(n_row, n_col, *args):
    (
        latent,
        logs,
        cond,
        trace,
        norm_gain,
        in_weight,
        conv,
        bc,
        dt,
        dt_bias,
        row_rate,
        col_rate,
        horizon,
        out_gain,
        out_weight,
    ) = args
    rows, cols, width = latent.shape
    inner = in_weight.shape[1] // 2
    cells = rows * cols
    count = n_row * n_col
    per = logs.shape[0]
    vmem = pl.BlockSpec(memory_space=pltpu.VMEM)
    operands = (
        latent,
        logs,
        cond,
        trace,
        norm_gain.reshape(1, width),
        in_weight,
        conv,
        bc,
        dt.T,
        dt_bias,
        row_rate,
        col_rate,
        horizon.T,
        out_gain.reshape(1, inner),
        out_weight,
    )
    own = [pltpu.VMEM(one.shape, one.dtype) for one in operands]
    own[3] = pltpu.SMEM(trace.shape, trace.dtype)
    dma = pltpu.SemaphoreType.DMA
    return pl.pallas_call(
        functools.partial(kernel, n_row, n_col),
        out_shape=jax.ShapeDtypeStruct((rows, cols, width), F32),
        in_specs=[pl.BlockSpec(memory_space=pltpu.HBM)] * len(operands),
        out_specs=vmem,
        scratch_shapes=own
        + [
            dma((len(operands),)),
            pltpu.VMEM((9, cells, cells + 6 * cols + 2 * rows), BF16),
            pltpu.VMEM((4, cells, (levels(max(rows, cols)) + 1) * cells), BF16),
            pltpu.VMEM((2 * levels(rows) + 2 * levels(cols) + 1, cells, cells), BF16),
            pltpu.VMEM((2, 3, cells, cells), BF16),
            pltpu.VMEM((rows, cols, width), F32),
            pltpu.VMEM((per, width), F32),
            pltpu.VMEM((count, per, width), F32),
            pltpu.VMEM((count * per, width), F32),
            pltpu.VMEM((cols, count * per), F32),
            pltpu.VMEM((2, cols, count * per), F32),
            pltpu.VMEM((2, rows, width), F32),
            pltpu.VMEM((6, cols, width), F32),
            pltpu.VMEM((2, rows, width), F32),
            pltpu.VMEM((n_col, 1, cells), F32),
            pltpu.VMEM((n_row, 1, cells), F32),
            pltpu.VMEM((n_col, cells, inner), BF16),
            pltpu.VMEM((n_row, cells, inner), BF16),
            dma,
            dma,
            dma((10,)),
            dma((10,)),
            dma((n_col,)),
            dma((n_col,)),
            dma((n_row,)),
            dma((n_row,)),
            dma((n_col,)),
            dma((n_col,)),
            dma((n_col // 2,)),
            dma((n_col // 2,)),
            dma((n_row,)),
            dma((n_row,)),
        ],
        compiler_params=pltpu.CompilerParams(
            collective_id=0, has_side_effects=True, vmem_limit_bytes=VMEM_LIMIT
        ),
    )(*operands).astype(BF16)


def solution(mesh):
    placed = (
        P("row", "col", None),
        P(("row", "col"), None),
        P(),
        P("col"),
        P(),
        P(),
        P(),
        P(),
        P(),
        P(),
        P(),
        P(),
        P("row", "col"),
        P(),
        P(),
    )
    return jax.shard_map(
        functools.partial(per_device, mesh.shape["row"], mesh.shape["col"]),
        mesh=mesh,
        in_specs=placed,
        out_specs=P("row", "col", None),
        check_vma=False,
    )
```
